32 devices in a mesh: inp: 4 (over x, core), chan: 8 (over z, y).
Axes of the slice: x: 2, y: 2, z: 4, core: 2. Of those that a mesh axis runs over, the one named last changes fastest.
Arguments:
- voltages: bfloat16 [2, 512, 77824], P(None, ('inp', 'chan')), may hold values from -6 to 6
- filter_taps: float32 [16, 4096], replicated, may hold values from -1.5 to 1.5
- pairing: int32 [3], replicated, may hold values from 1 to 3, as said below
Outputs:
- visibilities: float32 [2, 3, 32, 512, 128], P(None, None, 'chan', 'inp')
- autos: float32 [2, 64, 512, 128], P(None, 'chan', 'inp')
The draws below stay inside these ranges and needn't reach their ends.
Inputs may be any that keep to these rules, and one draw needn't show every extreme that they name: Every value from 1 to 3 appears exactly once; in round r block a is paired with block a XOR pairing[r].
All inputs are finite; a program needn't handle non-finite values.
Results may differ from the reference program's by a relative error of at most 0.004.
Values may be sent and summed in bfloat16 or wider, within the bound.
No kernel may reach another device: no remote copies, remote signals or barrier semaphores. Data moves between devices by JAX's collectives and lax.ppermute only.
A program may use at most 64 MiB of HBM per device.

```python
import jax
import jax.numpy as jnp
from jax import lax

FINE = 4096
TAPS = 16
SIG_BLK = 128
AVG = 64
SPEC = 4
BLOCKS = 4
ROUNDS = 3
SIGNALS = 512
SAMPLES = 77824
OUT_HALF = 32
OUT_ALL = 64
N_CHAN = 8


def draw_pairing(key, part):
    return (jax.random.permutation(key, BLOCKS - 1) + 1).astype(jnp.int32)


def block_scale(stream_key, extent, split, smallest, largest):
    loudness = 1.0
    for axis_at, blocks in split:
        steps = jax.random.uniform(jax.random.fold_in(jax.random.fold_in(stream_key, 6), axis_at), (blocks,), jnp.float32, smallest / len(split), largest / len(split))
        loudness = loudness * jnp.repeat(jnp.exp(steps), extent[axis_at] // blocks).reshape((-1,) + (1,) * (len(extent) - 1 - axis_at))
    return loudness


def normal_values(rng, extent, deviation, reach, split=(), held_as=jnp.bfloat16):
    entries = deviation * jax.random.normal(rng, extent, jnp.float32)
    if split:
        entries = entries * block_scale(rng, extent, split, -0.22, 0.18)
    return jnp.clip(entries, -reach, reach).astype(held_as)


def setup_inputs(seed: int = 0) -> dict:
    arg_keys = jax.random.split(jax.random.key(seed), 4)
    voltages = normal_values(arg_keys[0], (2, SIGNALS, SAMPLES), 1.0, 6.0, ((1, 32),))
    filter_taps = normal_values(arg_keys[1], (TAPS, FINE), 0.25, 1.5, (), jnp.float32)
    pairing = draw_pairing(jax.random.fold_in(arg_keys[3], 71), 0)
    return dict(voltages=voltages, filter_taps=filter_taps, pairing=pairing)


def spectra_of(volt_rows, filter_taps):
    count = volt_rows.shape[1]
    frames = volt_rows.astype(jnp.float32).reshape(2, count, SPEC + TAPS - 1, FINE)
    filtered = filter_taps[0] * frames[:, :, 0:SPEC, :]
    for tap_index in range(1, TAPS):
        filtered = filtered + filter_taps[tap_index] * frames[:, :, tap_index:tap_index + SPEC, :]
    complex_rows = filtered[0] + 1j * filtered[1]
    transformed = jnp.fft.fft(complex_rows, axis=-1) * (FINE ** -0.5)
    return jnp.stack([jnp.real(transformed), jnp.imag(transformed)]).astype(jnp.bfloat16)


def correlate(left_side, right_side):
    groups = left_side.shape[3] // AVG
    left_rows = left_side.astype(jnp.float32).reshape(2, SIG_BLK, SPEC, groups, AVG)
    right_rows = right_side.astype(jnp.float32).reshape(2, SIG_BLK, SPEC, groups, AVG)
    real_part = jnp.einsum('isgc,jsgc->gij', left_rows[0], right_rows[0]) + jnp.einsum('isgc,jsgc->gij', left_rows[1], right_rows[1])
    imag_part = jnp.einsum('isgc,jsgc->gij', left_rows[1], right_rows[0]) - jnp.einsum('isgc,jsgc->gij', left_rows[0], right_rows[1])
    return jnp.stack([real_part, imag_part]) / (SPEC * AVG)


def reference(voltages, filter_taps, pairing):
    block_ids = jnp.arange(BLOCKS, dtype=jnp.int32)

    def one_block(block_index):
        rows = lax.dynamic_slice_in_dim(voltages, (block_index * SIG_BLK).astype(jnp.int32), SIG_BLK, 1)
        return spectra_of(rows, filter_taps)

    spectra = lax.map(one_block, block_ids)
    autos = lax.map(lambda rows: correlate(rows, rows), spectra)
    autos = autos.transpose(1, 2, 0, 3, 4).reshape(2, OUT_ALL, SIGNALS, SIG_BLK)

    def pick_half(rows, upper):
        shaped = rows.reshape(2, SIG_BLK, SPEC, N_CHAN, 2, FINE // N_CHAN // 2)
        chosen = lax.dynamic_index_in_dim(shaped, upper, 4, keepdims=False)
        return chosen.reshape(2, SIG_BLK, SPEC, FINE // 2)

    rounds_out = []
    for round_index in range(ROUNDS):
        mask_value = pairing[round_index]

        def per_block(own_index):
            partner = jnp.bitwise_xor(own_index, mask_value).astype(jnp.int32)
            upper = (own_index > partner).astype(jnp.int32)
            own_rows = lax.dynamic_index_in_dim(spectra, own_index, 0, keepdims=False)
            other_rows = lax.dynamic_index_in_dim(spectra, partner, 0, keepdims=False)
            return correlate(pick_half(own_rows, upper), pick_half(other_rows, upper))

        result = lax.map(per_block, block_ids)
        rounds_out.append(result.transpose(1, 2, 0, 3, 4).reshape(2, OUT_HALF, SIGNALS, SIG_BLK))
    visibilities = jnp.stack(rounds_out, axis=1)
    return visibilities, autos
```

```python
import functools
import math

import jax
import jax.numpy as jnp
import numpy as np
from jax import lax
from jax.experimental import pallas as pl
from jax.experimental.pallas import tpu as pltpu
from jax.sharding import PartitionSpec as P

AVG = 64
LANES = 128
OUTER = 32
ROWS = 16
VMEM_LIMIT = 56 * 1024 * 1024


def twiddle_table():
    fine = OUTER * LANES
    k1 = np.arange(OUTER)[None, :, None]
    odd = np.arange(2)[:, None, None]
    q = np.arange(LANES)[None, None, :]
    turned = k1 + OUTER * ((-4 * k1 - 2 * odd) % LANES)
    angle = (turned * q % fine) * (2.0 * math.pi / fine)
    return np.stack([np.cos(angle), np.sin(angle)], axis=1).astype(np.float32)


def lane_matrix():
    fine = OUTER * LANES
    q = np.arange(LANES)
    angle = (q[:, None] * q[None, :] % LANES) * (2.0 * math.pi / LANES)
    cos, sin = np.cos(angle), np.sin(angle)
    full = (np.block([[cos, -sin], [sin, cos]]) * fine**-0.5).astype(np.float32)
    high = full.astype(jnp.bfloat16)
    low = (full - high.astype(np.float32)).astype(jnp.bfloat16)
    return np.stack([high, low])


def add(x, y):
    return (x[0] + y[0], x[1] + y[1])


def sub(x, y):
    return (x[0] - y[0], x[1] - y[1])


def minus_i(x):
    return (x[1], -x[0])


def turn(x, step, count):
    step %= count
    if step == 0:
        return x
    if 4 * step == count:
        return minus_i(x)
    if 8 * step == count:
        half = math.sqrt(0.5)
        return ((x[0] + x[1]) * half, (x[1] - x[0]) * half)
    if 8 * step == 3 * count:
        half = math.sqrt(0.5)
        return ((x[1] - x[0]) * half, (x[0] + x[1]) * -half)
    cos, sin = math.cos(2 * math.pi * step / count), math.sin(2 * math.pi * step / count)
    return (x[0] * cos + x[1] * sin, x[1] * cos - x[0] * sin)


def four(x):
    even, odd = add(x[0], x[2]), sub(x[0], x[2])
    other, last = add(x[1], x[3]), minus_i(sub(x[1], x[3]))
    return [add(even, other), add(odd, last), sub(even, other), sub(odd, last)]


def eight(x):
    even, odd = four(x[0::2]), four(x[1::2])
    odd = [turn(value, k, 8) for k, value in enumerate(odd)]
    return [add(e, o) for e, o in zip(even, odd)] + [sub(e, o) for e, o in zip(even, odd)]


def spectra_kernel(
    chan_count, spectra_count, volt_ref, taps_ref, twist_ref, matrix_ref, *refs
):
    outs = refs[:chan_count]
    filtered, first, last, pieces, sems = refs[chan_count:]
    tap_count, fine = taps_ref.shape
    frame_count = spectra_count + tap_count - 1

    def filter_column(p, carry):
        column = pl.multiple_of(p * LANES, LANES)
        taps = [taps_ref[pl.ds(t, 1), pl.ds(column, LANES)] for t in range(tap_count)]
        for part in range(2):
            sums = [None] * spectra_count
            for frame in range(frame_count):
                at = pl.multiple_of(frame * fine + column, LANES)
                values = volt_ref[part, :, pl.ds(at, LANES)].astype(jnp.float32)
                for s in range(spectra_count):
                    t = frame - s
                    if 0 <= t < tap_count:
                        term = taps[t] * values
                        sums[s] = term if sums[s] is None else sums[s] + term
            for s in range(spectra_count):
                filtered[s, part, p] = sums[s]
        return carry

    lax.fori_loop(0, OUTER, filter_column, 0)

    def transform(s, carry):
        for a in range(8):
            values = four([(filtered[s, 0, a + 8 * b], filtered[s, 1, a + 8 * b]) for b in range(4)])
            for r in range(4):
                real, imag = turn(values[r], a * r, OUTER)
                first[0, r, a] = real
                first[1, r, a] = imag
        odd = lax.rem(s, 2)
        for r in range(4):
            values = eight([(first[0, r, a], first[1, r, a]) for a in range(8)])
            highs, lows = [], []
            for t in range(8):
                k1 = r + 4 * t
                cos = twist_ref[odd, 0, pl.ds(k1, 1), :]
                sin = twist_ref[odd, 1, pl.ds(k1, 1), :]
                real, imag = values[t]
                row = jnp.concatenate([real * cos + imag * sin, imag * cos - real * sin], axis=1)
                high = row.astype(jnp.bfloat16)
                highs.append(high)
                lows.append((row - high.astype(jnp.float32)).astype(jnp.bfloat16))
            high = jnp.concatenate(highs, axis=0)
            low = jnp.concatenate(lows, axis=0)
            dot = functools.partial(jnp.dot, preferred_element_type=jnp.float32)
            result = dot(high, matrix_ref[0]) + (dot(low, matrix_ref[0]) + dot(high, matrix_ref[1]))
            result = result.astype(jnp.bfloat16)
            for t in range(8):
                rows = result[t * ROWS : (t + 1) * ROWS]
                last[s, 0, r + 4 * t] = rows[:, :LANES]
                last[s, 1, r + 4 * t] = rows[:, LANES:]
        return carry

    lax.fori_loop(0, spectra_count, transform, 0)

    lane = lax.broadcasted_iota(jnp.int32, (ROWS, LANES), 1)
    bits = [(lane >> bit) & 1 == 1 for bit in range(7)]
    group_count = pieces.shape[1]

    def regroup(part, carry):
        for pair in range(spectra_count // 2):
            even = [last[2 * pair, part, k1] for k1 in range(OUTER)]
            odd = [last[2 * pair + 1, part, k1] for k1 in range(OUTER)]
            mixed = [
                [jnp.where(bits[1], odd[v], even[v]) for v in range(OUTER)],
                [jnp.where(bits[1], even[v], odd[v - 1]) for v in range(OUTER)],
            ]
            for which in range(2):
                tiles = [mixed[which][-v % OUTER] for v in range(OUTER)]
                for bit in range(5):
                    tiles = [
                        jnp.where(bits[2 + bit], tiles[v - (1 << bit)], tiles[v])
                        for v in range(OUTER)
                    ]
                for u in range(OUTER):
                    chan, group = divmod(2 * u + which, group_count)
                    pieces[chan, group, part * (spectra_count // 2) + pair] = tiles[u]
        return carry

    lax.fori_loop(0, 2, regroup, 0)
    own = lax.axis_index("chan")
    copies = [
        pltpu.make_async_copy(pieces.at[jnp.bitwise_xor(own, k)], outs[k], sems.at[k])
        for k in range(chan_count)
    ]
    for copy in copies:
        copy.start()
    for copy in copies:
        copy.wait()


def spectra_pieces(voltages, filter_taps, chan_count):
    tap_count, fine = filter_taps.shape
    signals = voltages.shape[1]
    spectra_count = voltages.shape[2] // fine - tap_count + 1
    padded = -signals % ROWS
    if padded:
        voltages = jnp.pad(voltages, ((0, 0), (0, padded), (0, 0)))
    group_count = fine // AVG // chan_count
    slices = spectra_count
    piece = (group_count, slices, ROWS, LANES)
    outs = pl.pallas_call(
        functools.partial(spectra_kernel, chan_count, spectra_count),
        out_shape=[jax.ShapeDtypeStruct(piece, jnp.bfloat16)] * chan_count,
        in_specs=[pl.BlockSpec(memory_space=pltpu.VMEM)] * 4,
        out_specs=[pl.BlockSpec(memory_space=pl.ANY)] * chan_count,
        scratch_shapes=[
            pltpu.VMEM((spectra_count, 2, OUTER, ROWS, LANES), jnp.float32),
            pltpu.VMEM((2, 4, 8, ROWS, LANES), jnp.float32),
            pltpu.VMEM((spectra_count, 2, OUTER, ROWS, LANES), jnp.bfloat16),
            pltpu.VMEM((chan_count,) + piece, jnp.bfloat16),
            pltpu.SemaphoreType.DMA((chan_count,)),
        ],
        compiler_params=pltpu.CompilerParams(vmem_limit_bytes=VMEM_LIMIT),
        name="spectra",
    )(voltages, filter_taps, jnp.asarray(twiddle_table()), jnp.asarray(lane_matrix()))
    return [out[:, :, :signals] for out in outs]


def products(left, right):
    slices = left.shape[0]
    real_first = [left[i] for i in range(slices)]
    turned = real_first[slices // 2 :] + [-value for value in real_first[: slices // 2]]
    other = jnp.concatenate([right[i] for i in range(slices)], axis=1)
    contract = (((1,), (1,)), ((), ()))
    scale = 2.0 / (slices * LANES)
    results = []
    for side in (real_first, turned):
        rows = jnp.concatenate(side, axis=1)
        results.append(
            lax.dot_general(rows, other, contract, preferred_element_type=jnp.float32) * scale
        )
    return results


def autos_kernel(chan_count, inp_count, *refs):
    pieces = refs[:chan_count]
    block, autos, lower, upper = refs[chan_count:]
    own = lax.axis_index("chan")
    for k, piece in enumerate(pieces):
        source = jnp.bitwise_xor(own, k)
        rows = piece.shape[2]
        if rows == block.shape[2]:
            block[...] = piece[...]
        else:
            block[:, :, pl.ds(pl.multiple_of(source * rows, rows), rows), :] = piece[...]
    group_count = block.shape[0]
    half = group_count // 2
    lower[...] = block[:half]
    upper[...] = block[half:]

    def correlate(group, carry):
        rows = block[group]
        autos[0, group], autos[1, group] = products(rows, rows)
        return carry

    lax.fori_loop(0, group_count, correlate, 0)


def cross_kernel(order_ref, upper_ref, block, *refs):
    received = refs[:-1]
    visibilities = refs[-1]
    half = block.shape[0] // 2

    def correlate(group, carry):
        for index, other in enumerate(received):
            rows = block[upper_ref[index] * half + group]
            real, imag = products(rows, other[group])
            visibilities[0, order_ref[index], group] = real
            visibilities[1, order_ref[index], group] = imag
        return carry

    lax.fori_loop(0, half, correlate, 0)


def on_device(voltages, filter_taps, pairing):
    chan_count = lax.axis_size("chan")
    inp_count = lax.axis_size("inp")
    own_block = lax.axis_index("inp")

    def exchange(value, axis, mask):
        count = lax.axis_size(axis)
        return lax.ppermute(value, axis, [(i, i ^ mask) for i in range(count)])

    pieces = spectra_pieces(voltages, filter_taps, chan_count)
    pieces = [
        piece if k == 0 else exchange(piece, "chan", k) for k, piece in enumerate(pieces)
    ]
    group_count, slices, signals, _ = pieces[0].shape
    rows = signals * chan_count
    if signals % ROWS:
        order = jnp.bitwise_xor(lax.axis_index("chan"), jnp.arange(chan_count))
        whole = jnp.take(jnp.stack(pieces), order, axis=0)
        pieces = [whole.transpose(1, 2, 0, 3, 4).reshape(group_count, slices, rows, LANES)]
    half = group_count // 2
    block, autos, lower, upper = pl.pallas_call(
        functools.partial(autos_kernel, len(pieces), inp_count),
        out_shape=[
            jax.ShapeDtypeStruct((group_count, slices, rows, LANES), jnp.bfloat16),
            jax.ShapeDtypeStruct((2, group_count, rows, rows), jnp.float32),
            jax.ShapeDtypeStruct((half, slices, rows, LANES), jnp.bfloat16),
            jax.ShapeDtypeStruct((half, slices, rows, LANES), jnp.bfloat16),
        ],
        in_specs=[pl.BlockSpec(memory_space=pltpu.VMEM)] * len(pieces),
        out_specs=[pl.BlockSpec(memory_space=pltpu.VMEM)] * 4,
        compiler_params=pltpu.CompilerParams(vmem_limit_bytes=VMEM_LIMIT),
        name="autos",
    )(*pieces)
    masks = list(range(1, inp_count))
    is_upper = [(own_block >> (mask.bit_length() - 1)) & 1 for mask in masks]
    received = {}
    for mask, up in zip(masks, is_upper):
        if mask == 1 or mask % 2 == 0:
            received[mask] = exchange(jnp.where(up == 1, lower, upper), "inp", mask)
        else:
            received[mask] = exchange(received[mask - 1], "inp", 1)
    order = jnp.argmax(pairing[None, :] == jnp.array(masks, jnp.int32)[:, None], axis=1)
    visibilities = pl.pallas_call(
        cross_kernel,
        out_shape=jax.ShapeDtypeStruct((2, len(masks), half, rows, rows), jnp.float32),
        in_specs=[pl.BlockSpec(memory_space=pltpu.SMEM)] * 2
        + [pl.BlockSpec(memory_space=pltpu.VMEM)] * (1 + len(masks)),
        out_specs=pl.BlockSpec(memory_space=pltpu.VMEM),
        compiler_params=pltpu.CompilerParams(vmem_limit_bytes=VMEM_LIMIT),
        name="cross",
    )(
        order.astype(jnp.int32),
        jnp.stack(is_upper).astype(jnp.int32),
        block,
        *[received[mask] for mask in masks],
    )
    return (visibilities, autos)


def solution(mesh):
    in_specs = (P(None, ("inp", "chan"), None), P(), P())
    out_specs = (P(None, None, "chan", "inp", None), P(None, "chan", "inp", None))
    return jax.shard_map(
        on_device, mesh=mesh, in_specs=in_specs, out_specs=out_specs, check_vma=False
    )
```

```python
import functools
import math

import jax
import jax.numpy as jnp
import numpy as np
from jax import lax
from jax.experimental import pallas as pl
from jax.experimental.pallas import tpu as pltpu
from jax.sharding import PartitionSpec as P

AVG = 64
LANES = 128
OUTER = 32
ROWS = 16
MIB = 1024 * 1024


def twiddle_table():
    fine = OUTER * LANES
    k1 = np.arange(OUTER)[None, :, None]
    odd = np.arange(2)[:, None, None]
    q = np.arange(LANES)[None, None, :]
    turned = k1 + OUTER * ((-4 * k1 - 2 * odd) % LANES)
    angle = (turned * q % fine) * (2.0 * math.pi / fine)
    return np.concatenate([np.cos(angle), np.sin(angle)], axis=2).astype(np.float32)


def lane_matrix():
    fine = OUTER * LANES
    q = np.arange(LANES)
    angle = (q[:, None] * q[None, :] % LANES) * (2.0 * math.pi / LANES)
    cos, sin = np.cos(angle), np.sin(angle)
    return (np.block([[cos, -sin], [sin, cos]]) * fine**-0.5).astype(np.float32)


def add(x, y):
    return (x[0] + y[0], x[1] + y[1])


def sub(x, y):
    return (x[0] - y[0], x[1] - y[1])


def minus_i(x):
    return (x[1], -x[0])


def turn(x, step, count):
    step %= count
    if step == 0:
        return x
    if 4 * step == count:
        return minus_i(x)
    if 8 * step == count:
        half = math.sqrt(0.5)
        return ((x[0] + x[1]) * half, (x[1] - x[0]) * half)
    if 8 * step == 3 * count:
        half = math.sqrt(0.5)
        return ((x[1] - x[0]) * half, (x[0] + x[1]) * -half)
    cos, sin = math.cos(2 * math.pi * step / count), math.sin(2 * math.pi * step / count)
    return (x[0] * cos + x[1] * sin, x[1] * cos - x[0] * sin)


def four(x):
    even, odd = add(x[0], x[2]), sub(x[0], x[2])
    other, last = add(x[1], x[3]), minus_i(sub(x[1], x[3]))
    return [add(even, other), add(odd, last), sub(even, other), sub(odd, last)]


def eight(x):
    even, odd = four(x[0::2]), four(x[1::2])
    odd = [turn(value, k, 8) for k, value in enumerate(odd)]
    return [add(e, o) for e, o in zip(even, odd)] + [sub(e, o) for e, o in zip(even, odd)]


def bit_of(value, bit):
    return lax.rem(lax.div(value, 1 << bit), 2)


def top_bit(count):
    return count.bit_length() - 1


def spectra_kernel(chan_count, spectra_count, volt_hbm, taps_hbm, table_hbm, *refs):
    outs, scratch = refs[:-10], refs[-10:]
    volt_ref, taps_ref, table_ref, matrix_ref = scratch[:4]
    filtered, first, last, pieces, volt_sems, table_sems = scratch[4:]
    tap_count, fine = taps_ref.shape
    frame_count = spectra_count + tap_count - 1
    volt_copies = [
        pltpu.make_async_copy(volt_hbm.at[part], volt_ref.at[part], volt_sems.at[part])
        for part in range(2)
    ]
    table_copies = [
        pltpu.make_async_copy(source, target, table_sems.at[at])
        for at, (source, target) in enumerate(
            [(taps_hbm, taps_ref), (table_hbm, table_ref)]
        )
    ]
    table_copies[0].start()
    volt_copies[0].start()
    volt_copies[1].start()
    table_copies[1].start()
    table_copies[0].wait()
    for part in range(2):
        volt_copies[part].wait()

        def filter_column(p, carry, part=part):
            column = pl.multiple_of(p * LANES, LANES)
            taps = [taps_ref[pl.ds(t, 1), pl.ds(column, LANES)] for t in range(tap_count)]
            sums = [None] * spectra_count
            for frame in range(frame_count):
                at = pl.multiple_of(frame * fine + column, LANES)
                values = volt_ref[part, :, pl.ds(at, LANES)].astype(jnp.float32)
                for s in range(spectra_count):
                    t = frame - s
                    if 0 <= t < tap_count:
                        term = taps[t] * values
                        sums[s] = term if sums[s] is None else sums[s] + term
            for s in range(spectra_count):
                filtered[s, part, p] = sums[s]
            return carry

        lax.fori_loop(0, OUTER, filter_column, 0)
    table_copies[1].wait()
    table = table_ref[pl.ds(0, 2 * LANES), :]
    matrix_ref[0] = table.astype(jnp.bfloat16)
    matrix_ref[1] = (table - matrix_ref[0].astype(jnp.float32)).astype(jnp.bfloat16)

    def transform(s, carry):
        for a in range(8):
            values = four([(filtered[s, 0, a + 8 * b], filtered[s, 1, a + 8 * b]) for b in range(4)])
            for r in range(4):
                real, imag = turn(values[r], a * r, OUTER)
                first[0, r, a] = real
                first[1, r, a] = imag
        odd = lax.rem(s, 2)
        for r in range(4):
            values = eight([(first[0, r, a], first[1, r, a]) for a in range(8)])
            highs, lows = [], []
            for t in range(8):
                k1 = r + 4 * t
                factors = table_ref[pl.ds(2 * LANES + odd * OUTER + k1, 1), :]
                cos, sin = factors[:, :LANES], factors[:, LANES:]
                real, imag = values[t]
                row = jnp.concatenate([real * cos + imag * sin, imag * cos - real * sin], axis=1)
                high = row.astype(jnp.bfloat16)
                highs.append(high)
                lows.append((row - high.astype(jnp.float32)).astype(jnp.bfloat16))
            high = jnp.concatenate(highs, axis=0)
            low = jnp.concatenate(lows, axis=0)
            dot = functools.partial(jnp.dot, preferred_element_type=jnp.float32)
            result = dot(high, matrix_ref[0]) + (dot(low, matrix_ref[0]) + dot(high, matrix_ref[1]))
            result = result.astype(jnp.bfloat16)
            for t in range(8):
                rows = result[t * ROWS : (t + 1) * ROWS]
                last[s, 0, r + 4 * t] = rows[:, :LANES]
                last[s, 1, r + 4 * t] = rows[:, LANES:]
        return carry

    lax.fori_loop(0, spectra_count, transform, 0)

    lane = lax.broadcasted_iota(jnp.int32, (ROWS, LANES), 1)
    bits = [(lane >> bit) & 1 == 1 for bit in range(7)]
    group_count = pieces.shape[1]

    def regroup(part, carry):
        for pair in range(spectra_count // 2):
            even = [last[2 * pair, part, k1] for k1 in range(OUTER)]
            odd = [last[2 * pair + 1, part, k1] for k1 in range(OUTER)]
            mixed = [
                [jnp.where(bits[1], odd[v], even[v]) for v in range(OUTER)],
                [jnp.where(bits[1], even[v], odd[v - 1]) for v in range(OUTER)],
            ]
            for which in range(2):
                tiles = [mixed[which][-v % OUTER] for v in range(OUTER)]
                for bit in range(5):
                    tiles = [
                        jnp.where(bits[2 + bit], tiles[v - (1 << bit)], tiles[v])
                        for v in range(OUTER)
                    ]
                for u in range(OUTER):
                    chan, group = divmod(2 * u + which, group_count)
                    pieces[chan, group, part * (spectra_count // 2) + pair] = tiles[u]
        return carry

    lax.fori_loop(0, 2, regroup, 0)
    own = lax.axis_index("chan")
    top = bit_of(lax.axis_index("inp"), top_bit(lax.axis_size("inp")) - 1)
    half = group_count // 2
    moving, other = pl.ds((1 - top) * half, half), pl.ds(top * half, half)
    own_moving, own_other, *direct, held, relay_moving, relay_other = outs
    own_moving[...] = pieces[own, moving]
    own_other[...] = pieces[own, other]
    for index in range(chan_count // 2):
        chan = jnp.bitwise_xor(own, 2 * index)
        if index:
            direct[index - 1][...] = pieces[chan, moving]
            held[index - 1] = pieces[chan, other]
        relay_moving[index] = pieces[jnp.bitwise_xor(chan, 1), moving]
        relay_other[index] = pieces[jnp.bitwise_xor(chan, 1), other]


def spectra_pieces(voltages, filter_taps, chan_count):
    tap_count, fine = filter_taps.shape
    signals = voltages.shape[1]
    spectra_count = voltages.shape[2] // fine - tap_count + 1
    padded = -signals % ROWS
    if padded:
        voltages = jnp.pad(voltages, ((0, 0), (0, padded), (0, 0)))
    group_count = fine // AVG // chan_count
    slices = spectra_count
    piece = (group_count, slices, ROWS, LANES)
    part = (group_count // 2, slices, ROWS, LANES)
    half_count = chan_count // 2
    shapes = [part] * (half_count + 1) + [(half_count - 1,) + part] + [(half_count,) + part] * 2
    table = np.concatenate([lane_matrix(), twiddle_table().reshape(-1, 2 * LANES)])
    outs = pl.pallas_call(
        functools.partial(spectra_kernel, chan_count, spectra_count),
        out_shape=[jax.ShapeDtypeStruct(shape, jnp.bfloat16) for shape in shapes],
        in_specs=[pl.BlockSpec(memory_space=pltpu.HBM)] * 3,
        out_specs=[pl.BlockSpec(memory_space=pltpu.VMEM)] * len(shapes),
        scratch_shapes=[
            pltpu.VMEM(voltages.shape, jnp.bfloat16),
            pltpu.VMEM(filter_taps.shape, jnp.float32),
            pltpu.VMEM(table.shape, jnp.float32),
            pltpu.VMEM((2, 2 * LANES, 2 * LANES), jnp.bfloat16),
            pltpu.VMEM((spectra_count, 2, OUTER, ROWS, LANES), jnp.float32),
            pltpu.VMEM((2, 4, 8, ROWS, LANES), jnp.float32),
            pltpu.VMEM((spectra_count, 2, OUTER, ROWS, LANES), jnp.bfloat16),
            pltpu.VMEM((chan_count,) + piece, jnp.bfloat16),
            pltpu.SemaphoreType.DMA((2,)),
            pltpu.SemaphoreType.DMA((2,)),
        ],
        compiler_params=pltpu.CompilerParams(vmem_limit_bytes=53 * MIB),
        name="spectra",
    )(voltages, filter_taps, jnp.asarray(table))
    outs = [out[..., :signals, :] for out in outs]
    return outs[:2] + [outs[2:-3]] + outs[-3:]


def vmem_call(name, kernel, out_shapes, operands, after=()):
    count = len(operands)
    operands = list(operands) + list(after)

    def body(*refs):
        kernel(*refs[:count], *refs[len(operands) :])

    return pl.pallas_call(
        body,
        out_shape=[jax.ShapeDtypeStruct(shape, jnp.bfloat16) for shape in out_shapes],
        in_specs=[pl.BlockSpec(memory_space=pltpu.VMEM)] * count
        + [pl.BlockSpec(memory_space=pl.ANY)] * len(after),
        out_specs=[pl.BlockSpec(memory_space=pltpu.VMEM)] * len(out_shapes),
        compiler_params=pltpu.CompilerParams(vmem_limit_bytes=8 * MIB),
        name=name,
    )(*operands)


def split_kernel(relayed, *outs):
    for index, out in enumerate(outs):
        out[...] = relayed[index + 1]


def hand_on_kernel(held, relayed, *outs):
    for index, out in enumerate(outs):
        out[0] = held[index]
        out[1] = relayed[index + 1]


def lay(out, pieces):
    count = len(pieces)
    if count == 1:
        out[...] = pieces[0][...]
        return
    own = lax.axis_index("chan")
    rows = out.shape[2] // count
    for k, piece in enumerate(pieces):
        source = jnp.bitwise_xor(lax.div(own, 2), k)
        span = pl.ds(pl.multiple_of(source * rows, rows), rows)
        out[:, :, span, :] = piece[...]


def lay_kernel(*refs):
    lay(refs[-1], refs[:-1])


def lay_relayed_kernel(relayed, *refs):
    lay(refs[-1], [relayed.at[0], *refs[:-1]])


def lay_rest_kernel(rest_count, near_moving, far_moving, own_other, relayed, *refs):
    rest, outs = refs[:rest_count], refs[rest_count:]
    near = [own_other] + [value.at[0] for value in rest]
    far = [relayed.at[0]] + [value.at[1] for value in rest]
    lay_other_kernel(len(near), near_moving, far_moving, *near, *far, *outs)


def lay_other_kernel(piece_count, near_moving, far_moving, *refs):
    near, far = refs[:piece_count], refs[piece_count : 2 * piece_count]
    near_other, far_other, *sends = refs[2 * piece_count :]
    lay(near_other, near)
    lay(far_other, far)
    block = lax.axis_index("inp")
    top = bit_of(block, len(sends))
    for bit, out in enumerate(sends):
        same = bit_of(block, bit) == top

        @pl.when(same)
        def _(out=out):
            out[0] = near_moving[...]
            out[1] = far_moving[...]

        @pl.when(jnp.logical_not(same))
        def _(out=out):
            out[0] = near_other[...]
            out[1] = far_other[...]


def products(left, right):
    slices = left.shape[0]
    real_first = [left[i] for i in range(slices)]
    turned = real_first[slices // 2 :] + [-value for value in real_first[: slices // 2]]
    other = jnp.concatenate([right[i] for i in range(slices)], axis=1)
    contract = (((1,), (1,)), ((), ()))
    scale = 2.0 / (slices * LANES)
    results = []
    for side in (real_first, turned):
        rows = jnp.concatenate(side, axis=1)
        results.append(
            lax.dot_general(rows, other, contract, preferred_element_type=jnp.float32) * scale
        )
    return results


def fill(target, parts, chan_count):
    if len(parts) == 1:
        target[...] = parts[0][...]
        return
    own = lax.rem(lax.axis_index("chan"), 2)
    rows = target.shape[2] // chan_count
    for parity, part in enumerate(parts):
        first = own if parity == 0 else 1 - own
        for source in range(chan_count // 2):
            span = pl.ds(pl.multiple_of((2 * source + first) * rows, rows), rows)
            target[:, :, span, :] = part[:, :, pl.ds(source * rows, rows), :]


def correlate_kernel(chan_count, block_bits, masks, layout, with_autos, pairing_ref, *refs):
    inputs = []
    at = 0
    for kind in layout:
        if kind == "stack":
            inputs.append([refs[at].at[0], refs[at].at[1]])
            at += 1
        else:
            count = 2 if kind == "pair" else 1
            inputs.append(list(refs[at : at + count]))
            at += count
    if not with_autos:
        at += 1
    refs = refs[at:]
    vis_hbm, refs = refs[0], refs[1:]
    if with_autos:
        autos_hbm, block, others, vis, vis_sems, autos, auto_sems = refs
    else:
        block, others, vis, vis_sems = refs
    top = bit_of(lax.axis_index("inp"), block_bits - 1)
    half = block.shape[1]
    for slot in range(2):
        fill(block.at[slot], inputs[slot], chan_count)
    for index in range(len(masks)):
        fill(others.at[index], inputs[2 + index], chan_count)
    places = []
    for mask in masks:
        at = jnp.int32(0)
        for turn_at in range(pairing_ref.shape[0]):
            at = jnp.where(pairing_ref[turn_at] == mask, turn_at, at)
        places.append(at)
    copies = []

    def store(source, target, sem):
        copy = pltpu.make_async_copy(source, target, sem)
        copy.start()
        copies.append(copy)

    for group in range(half):
        for index, mask in enumerate(masks):
            bit = top_bit(mask)
            slot = 1
            if bit != block_bits - 1:
                slot = (bit_of(lax.axis_index("inp"), bit) == top).astype(jnp.int32)
            left = block[slot, group]
            vis[0, index, group], vis[1, index, group] = products(left, others[index, group])
            for part in range(2):
                store(
                    vis.at[part, index, group],
                    vis_hbm.at[part, places[index], group],
                    vis_sems.at[part, index, group],
                )
        for slot in range(2 * with_autos):
            left = block[slot, group]
            at = half * (slot * top + (1 - slot) * (1 - top)) + group
            autos[0, slot, group], autos[1, slot, group] = products(left, left)
            for part in range(2):
                store(
                    autos.at[part, slot, group],
                    autos_hbm.at[part, at],
                    auto_sems.at[part, slot, group],
                )
    for copy in copies:
        copy.wait()


def correlate(pairing, entries, masks, chan_count, block_bits, before=None):
    half, slices, rows = entries[0][1][0].shape[-4:-1]
    operands, layout = [], []
    for kind, values in entries:
        layout.append(kind)
        operands += values
    if layout[0] != "whole":
        rows *= 2
    with_autos = before is None
    round_count = pairing.shape[0]
    vis_shape = (2, len(masks), half, rows, rows)
    auto_shape = (2, 2, half, rows, rows)
    outs = [jax.ShapeDtypeStruct((2, round_count, half, rows, rows), jnp.float32)]
    scratch = [
        pltpu.VMEM((2, half, slices, rows, LANES), jnp.bfloat16),
        pltpu.VMEM((len(masks), half, slices, rows, LANES), jnp.bfloat16),
        pltpu.VMEM(vis_shape, jnp.float32),
        pltpu.SemaphoreType.DMA(vis_shape[:3]),
    ]
    specs = [pl.BlockSpec(memory_space=pltpu.SMEM)]
    specs += [pl.BlockSpec(memory_space=pltpu.VMEM)] * len(operands)
    aliases = {}
    if with_autos:
        outs.append(jax.ShapeDtypeStruct((2, 2 * half, rows, rows), jnp.float32))
        scratch += [pltpu.VMEM(auto_shape, jnp.float32), pltpu.SemaphoreType.DMA(auto_shape[:3])]
    else:
        aliases = {len(specs): 0}
        specs.append(pl.BlockSpec(memory_space=pltpu.HBM))
        operands = operands + [before]
    flops = 16 * len(masks) * half * rows * rows * slices * LANES
    return pl.pallas_call(
        functools.partial(
            correlate_kernel, chan_count, block_bits, masks, tuple(layout), with_autos
        ),
        out_shape=outs,
        in_specs=specs,
        out_specs=[pl.BlockSpec(memory_space=pltpu.HBM)] * len(outs),
        scratch_shapes=scratch,
        input_output_aliases=aliases,
        compiler_params=pltpu.CompilerParams(vmem_limit_bytes=24 * MIB),
        cost_estimate=pl.CostEstimate(flops=flops, bytes_accessed=4 << 20, transcendentals=0),
        name="correlate" if with_autos else "correlate_rest",
    )(pairing, *operands)


def on_device(voltages, filter_taps, pairing):
    chan_count = lax.axis_size("chan")
    inp_count = lax.axis_size("inp")
    block_bits = top_bit(inp_count)
    own_chan = lax.axis_index("chan")
    signals = voltages.shape[1]

    def exchange(value, axis, mask):
        count = lax.axis_size(axis)
        return lax.ppermute(value, axis, [(i, i ^ mask) for i in range(count)])

    evens = list(range(2, chan_count, 2))
    own_moving, own_other, direct, held, relay_moving, relay_other = spectra_pieces(
        voltages, filter_taps, chan_count
    )
    part = own_moving.shape
    half = part[0]
    relay_moving = exchange(relay_moving, "chan", 1)
    direct = [exchange(value, "chan", k) for value, k in zip(direct, evens)]
    relay_other = exchange(relay_other, "chan", 1)
    onward = vmem_call(
        "split", split_kernel, [part] * len(evens), [relay_moving], []
    )
    onward = [exchange(value, "chan", k) for value, k in zip(onward, evens)]
    near, far = [own_moving] + direct, [relay_moving[0]] + onward
    laid = part[:2] + (chan_count // 2 * signals, LANES)
    whole_tiles = signals % ROWS == 0
    if whole_tiles:
        (near,) = vmem_call("near", lay_kernel, [laid], near, [])
        (far,) = vmem_call("far", lay_relayed_kernel, [laid], [relay_moving] + onward, [])
    else:
        sources = jnp.bitwise_xor(own_chan // 2, jnp.arange(chan_count // 2))

        def merge(parts):
            return jnp.take(jnp.stack(parts, axis=2), sources, axis=2).reshape(laid)

        near, far = merge(near), merge(far)
    top_mask = inp_count // 2
    crossed = [exchange(value, "inp", top_mask) for value in (near, far)]
    rest = vmem_call(
        "hand_on",
        hand_on_kernel,
        [(2,) + part] * len(evens),
        [held, relay_other],
        [near],
    )
    rest = [exchange(value, "chan", k) for value, k in zip(rest, evens)]
    if whole_tiles:
        other_kernel = functools.partial(lay_rest_kernel, len(evens))
        others = [own_other, relay_other] + rest
    else:
        other_kernel = functools.partial(lay_other_kernel, 1)
        others = [
            merge([own_other] + [value[0] for value in rest]),
            merge([relay_other[0]] + [value[1] for value in rest]),
        ]
    near_other, far_other, *sends = vmem_call(
        "other",
        other_kernel,
        [laid] * 2 + [(2,) + laid] * (block_bits - 1),
        [near, far] + others,
        [],
    )
    masks = list(range(1, inp_count))
    received = {top_mask: ("pair", crossed)}
    for mask in masks:
        bit = top_bit(mask)
        if mask == top_mask:
            continue
        if mask > 1 and mask % 2:
            kind, values = received[mask - 1]
            received[mask] = (kind, [exchange(value, "inp", 1) for value in values])
        else:
            kind, values = "pair", [near, far]
            if bit != block_bits - 1:
                kind, values = "stack", [sends[bit]]
            received[mask] = (kind, [exchange(value, "inp", mask) for value in values])
    block = [("pair", [near, far]), ("pair", [near_other, far_other])]
    if not whole_tiles:
        parities = jnp.bitwise_xor(own_chan % 2, jnp.arange(2))

        def interleave(entry):
            kind, values = entry
            if kind == "stack":
                values = [values[0][0], values[0][1]]
            shaped = [value.reshape(half, -1, chan_count // 2, signals, LANES) for value in values]
            ordered = jnp.take(jnp.stack(shaped, axis=3), parities, axis=3)
            return ("whole", [ordered.reshape(half, -1, chan_count * signals, LANES)])

        block = [interleave(entry) for entry in block]
        received = {mask: interleave(entry) for mask, entry in received.items()}
    early = [mask for mask in masks if top_bit(mask) == block_bits - 1]
    late = [mask for mask in masks if top_bit(mask) != block_bits - 1]
    visibilities, autos = correlate(
        pairing, block + [received[mask] for mask in early], early, chan_count, block_bits
    )
    (visibilities,) = correlate(
        pairing,
        block + [received[mask] for mask in late],
        late,
        chan_count,
        block_bits,
        visibilities,
    )
    return (visibilities, autos)


def solution(mesh):
    in_specs = (P(None, ("inp", "chan"), None), P(), P())
    out_specs = (P(None, None, "chan", "inp", None), P(None, "chan", "inp", None))
    return jax.shard_map(
        on_device, mesh=mesh, in_specs=in_specs, out_specs=out_specs, check_vma=False
    )
```

```python
import functools
import math

import jax
import jax.numpy as jnp
import numpy as np
from jax import lax
from jax.experimental import pallas as pl
from jax.experimental.pallas import tpu as pltpu
from jax.sharding import PartitionSpec as P

AVG = 64
LANES = 128
OUTER = 32
ROWS = 16
MIB = 1024 * 1024


def twiddle_table():
    fine = OUTER * LANES
    k1 = np.arange(OUTER)[None, :, None]
    odd = np.arange(2)[:, None, None]
    q = np.arange(LANES)[None, None, :]
    turned = k1 + OUTER * ((-4 * k1 - 2 * odd) % LANES)
    angle = (turned * q % fine) * (2.0 * math.pi / fine)
    return np.concatenate([np.cos(angle), np.sin(angle)], axis=2).astype(np.float32)


def lane_matrix():
    fine = OUTER * LANES
    q = np.arange(LANES)
    angle = (q[:, None] * q[None, :] % LANES) * (2.0 * math.pi / LANES)
    cos, sin = np.cos(angle), np.sin(angle)
    return (np.block([[cos, -sin], [sin, cos]]) * fine**-0.5).astype(np.float32)


def add(x, y):
    return (x[0] + y[0], x[1] + y[1])


def sub(x, y):
    return (x[0] - y[0], x[1] - y[1])


def minus_i(x):
    return (x[1], -x[0])


def turn(x, step, count):
    step %= count
    if step == 0:
        return x
    if 4 * step == count:
        return minus_i(x)
    if 8 * step == count:
        half = math.sqrt(0.5)
        return ((x[0] + x[1]) * half, (x[1] - x[0]) * half)
    if 8 * step == 3 * count:
        half = math.sqrt(0.5)
        return ((x[1] - x[0]) * half, (x[0] + x[1]) * -half)
    cos, sin = math.cos(2 * math.pi * step / count), math.sin(2 * math.pi * step / count)
    return (x[0] * cos + x[1] * sin, x[1] * cos - x[0] * sin)


def four(x):
    even, odd = add(x[0], x[2]), sub(x[0], x[2])
    other, last = add(x[1], x[3]), minus_i(sub(x[1], x[3]))
    return [add(even, other), add(odd, last), sub(even, other), sub(odd, last)]


def eight(x):
    even, odd = four(x[0::2]), four(x[1::2])
    odd = [turn(value, k, 8) for k, value in enumerate(odd)]
    return [add(e, o) for e, o in zip(even, odd)] + [sub(e, o) for e, o in zip(even, odd)]


def bit_of(value, bit):
    return lax.rem(lax.div(value, 1 << bit), 2)


def top_bit(count):
    return count.bit_length() - 1


def hops(count):
    return [0] + sorted(range(2, count, 2), key=lambda hop: (-top_bit(hop), hop))


def spectra_kernel(chan_count, spectra_count, volt_hbm, taps_hbm, table_hbm, *refs):
    outs, scratch = refs[:-10], refs[-10:]
    volt_ref, taps_ref, table_ref, matrix_ref = scratch[:4]
    filtered, first, last, pieces, volt_sems, table_sems = scratch[4:]
    tap_count, fine = taps_ref.shape
    frame_count = spectra_count + tap_count - 1
    volt_copies = [
        pltpu.make_async_copy(volt_hbm.at[part], volt_ref.at[part], volt_sems.at[part])
        for part in range(2)
    ]
    table_copies = [
        pltpu.make_async_copy(source, target, table_sems.at[at])
        for at, (source, target) in enumerate(
            [(taps_hbm, taps_ref), (table_hbm, table_ref)]
        )
    ]
    table_copies[0].start()
    volt_copies[0].start()
    volt_copies[1].start()
    table_copies[1].start()
    table_copies[0].wait()
    for part in range(2):
        volt_copies[part].wait()

        def filter_column(p, carry, part=part):
            column = pl.multiple_of(p * LANES, LANES)
            taps = [taps_ref[pl.ds(t, 1), pl.ds(column, LANES)] for t in range(tap_count)]
            sums = [None] * spectra_count
            for frame in range(frame_count):
                at = pl.multiple_of(frame * fine + column, LANES)
                values = volt_ref[part, :, pl.ds(at, LANES)].astype(jnp.float32)
                for s in range(spectra_count):
                    t = frame - s
                    if 0 <= t < tap_count:
                        term = taps[t] * values
                        sums[s] = term if sums[s] is None else sums[s] + term
            for s in range(spectra_count):
                filtered[s, part, p] = sums[s]
            return carry

        lax.fori_loop(0, OUTER, filter_column, 0)
    table_copies[1].wait()
    table = table_ref[pl.ds(0, 2 * LANES), :]
    matrix_ref[0] = table.astype(jnp.bfloat16)
    matrix_ref[1] = (table - matrix_ref[0].astype(jnp.float32)).astype(jnp.bfloat16)

    def transform(s, carry):
        for a in range(8):
            values = four([(filtered[s, 0, a + 8 * b], filtered[s, 1, a + 8 * b]) for b in range(4)])
            for r in range(4):
                real, imag = turn(values[r], a * r, OUTER)
                first[0, r, a] = real
                first[1, r, a] = imag
        odd = lax.rem(s, 2)
        for r in range(4):
            values = eight([(first[0, r, a], first[1, r, a]) for a in range(8)])
            highs, lows = [], []
            for t in range(8):
                k1 = r + 4 * t
                factors = table_ref[pl.ds(2 * LANES + odd * OUTER + k1, 1), :]
                cos, sin = factors[:, :LANES], factors[:, LANES:]
                real, imag = values[t]
                row = jnp.concatenate([real * cos + imag * sin, imag * cos - real * sin], axis=1)
                high = row.astype(jnp.bfloat16)
                highs.append(high)
                lows.append((row - high.astype(jnp.float32)).astype(jnp.bfloat16))
            high = jnp.concatenate(highs, axis=0)
            low = jnp.concatenate(lows, axis=0)
            dot = functools.partial(jnp.dot, preferred_element_type=jnp.float32)
            result = dot(high, matrix_ref[0]) + (dot(low, matrix_ref[0]) + dot(high, matrix_ref[1]))
            result = result.astype(jnp.bfloat16)
            for t in range(8):
                rows = result[t * ROWS : (t + 1) * ROWS]
                last[s, 0, r + 4 * t] = rows[:, :LANES]
                last[s, 1, r + 4 * t] = rows[:, LANES:]
        return carry

    lax.fori_loop(0, spectra_count, transform, 0)

    lane = lax.broadcasted_iota(jnp.int32, (ROWS, LANES), 1)
    bits = [(lane >> bit) & 1 == 1 for bit in range(7)]
    group_count = pieces.shape[1]

    def regroup(part, carry):
        for pair in range(spectra_count // 2):
            even = [last[2 * pair, part, k1] for k1 in range(OUTER)]
            odd = [last[2 * pair + 1, part, k1] for k1 in range(OUTER)]
            mixed = [
                [jnp.where(bits[1], odd[v], even[v]) for v in range(OUTER)],
                [jnp.where(bits[1], even[v], odd[v - 1]) for v in range(OUTER)],
            ]
            for which in range(2):
                tiles = [mixed[which][-v % OUTER] for v in range(OUTER)]
                for bit in range(5):
                    tiles = [
                        jnp.where(bits[2 + bit], tiles[v - (1 << bit)], tiles[v])
                        for v in range(OUTER)
                    ]
                for u in range(OUTER):
                    chan, group = divmod(2 * u + which, group_count)
                    pieces[chan, group, part * (spectra_count // 2) + pair] = tiles[u]
        return carry

    lax.fori_loop(0, 2, regroup, 0)
    own = lax.axis_index("chan")
    top = bit_of(lax.axis_index("inp"), top_bit(lax.axis_size("inp")) - 1)
    half = group_count // 2
    moving, other = pl.ds((1 - top) * half, half), pl.ds(top * half, half)
    own_moving, own_other, *direct, held, relay_moving, relay_other = outs
    own_moving[...] = pieces[own, moving]
    own_other[...] = pieces[own, other]
    for index, hop in enumerate(hops(chan_count)):
        chan = jnp.bitwise_xor(own, hop)
        if index:
            direct[index - 1][...] = pieces[chan, moving]
            held[index - 1] = pieces[chan, other]
        relay_moving[index] = pieces[jnp.bitwise_xor(chan, 1), moving]
        relay_other[index] = pieces[jnp.bitwise_xor(chan, 1), other]


def spectra_pieces(voltages, filter_taps, chan_count):
    tap_count, fine = filter_taps.shape
    signals = voltages.shape[1]
    spectra_count = voltages.shape[2] // fine - tap_count + 1
    padded = -signals % ROWS
    if padded:
        voltages = jnp.pad(voltages, ((0, 0), (0, padded), (0, 0)))
    group_count = fine // AVG // chan_count
    slices = spectra_count
    piece = (group_count, slices, ROWS, LANES)
    part = (group_count // 2, slices, ROWS, LANES)
    half_count = chan_count // 2
    shapes = [part] * (half_count + 1) + [(half_count - 1,) + part] + [(half_count,) + part] * 2
    table = np.concatenate([lane_matrix(), twiddle_table().reshape(-1, 2 * LANES)])
    outs = pl.pallas_call(
        functools.partial(spectra_kernel, chan_count, spectra_count),
        out_shape=[jax.ShapeDtypeStruct(shape, jnp.bfloat16) for shape in shapes],
        in_specs=[pl.BlockSpec(memory_space=pltpu.HBM)] * 3,
        out_specs=[pl.BlockSpec(memory_space=pltpu.VMEM)] * len(shapes),
        scratch_shapes=[
            pltpu.VMEM(voltages.shape, jnp.bfloat16),
            pltpu.VMEM(filter_taps.shape, jnp.float32),
            pltpu.VMEM(table.shape, jnp.float32),
            pltpu.VMEM((2, 2 * LANES, 2 * LANES), jnp.bfloat16),
            pltpu.VMEM((spectra_count, 2, OUTER, ROWS, LANES), jnp.float32),
            pltpu.VMEM((2, 4, 8, ROWS, LANES), jnp.float32),
            pltpu.VMEM((spectra_count, 2, OUTER, ROWS, LANES), jnp.bfloat16),
            pltpu.VMEM((chan_count,) + piece, jnp.bfloat16),
            pltpu.SemaphoreType.DMA((2,)),
            pltpu.SemaphoreType.DMA((2,)),
        ],
        compiler_params=pltpu.CompilerParams(vmem_limit_bytes=53 * MIB),
        name="spectra",
    )(voltages, filter_taps, jnp.asarray(table))
    outs = [out[..., :signals, :] for out in outs]
    return outs[:2] + [outs[2:-3]] + outs[-3:]


def vmem_call(name, kernel, out_shapes, operands, after=(), cost=None, aliases=None):
    count = len(operands)
    operands = list(operands) + list(after)

    def body(*refs):
        kernel(*refs[:count], *refs[len(operands) :])

    return pl.pallas_call(
        body,
        out_shape=[jax.ShapeDtypeStruct(shape, jnp.bfloat16) for shape in out_shapes],
        in_specs=[pl.BlockSpec(memory_space=pltpu.VMEM)] * count
        + [pl.BlockSpec(memory_space=pl.ANY)] * len(after),
        out_specs=[pl.BlockSpec(memory_space=pltpu.VMEM)] * len(out_shapes),
        compiler_params=pltpu.CompilerParams(vmem_limit_bytes=8 * MIB),
        cost_estimate=cost,
        input_output_aliases=aliases or {},
        name=name,
    )(*operands)


def split_kernel(relayed, *outs):
    for index, out in enumerate(outs):
        out[...] = relayed[index]


def hand_on_kernel(held, relayed, *outs):
    for index, out in enumerate(outs):
        out[0] = held[index]
        out[1] = relayed[index + 1]


def lay(out, pieces):
    count = len(pieces)
    if count == 1:
        out[...] = pieces[0][...]
        return
    own = lax.axis_index("chan")
    rows = out.shape[2] // count
    for hop, piece in zip(hops(2 * count), pieces):
        source = lax.div(jnp.bitwise_xor(own, hop), 2)
        span = pl.ds(pl.multiple_of(source * rows, rows), rows)
        out[:, :, span, :] = piece[...]


def lay_kernel(*refs):
    lay(refs[-1], refs[:-1])


def lay_rest_kernel(rest_count, near_moving, far_moving, own_other, relayed, *refs):
    rest, outs = refs[:rest_count], refs[rest_count:]
    near = [own_other] + [value.at[0] for value in rest]
    far = [relayed.at[0]] + [value.at[1] for value in rest]
    lay_other_kernel(len(near), near_moving, far_moving, *near, *far, *outs)


def lay_other_kernel(piece_count, near_moving, far_moving, *refs):
    near, far = refs[:piece_count], refs[piece_count : 2 * piece_count]
    near_other, far_other, *sends = refs[2 * piece_count :]
    lay(near_other, near)
    lay(far_other, far)
    block = lax.axis_index("inp")
    top = bit_of(block, len(sends))
    for bit, out in enumerate(sends):
        same = bit_of(block, bit) == top

        @pl.when(same)
        def _(out=out):
            out[0] = near_moving[...]
            out[1] = far_moving[...]

        @pl.when(jnp.logical_not(same))
        def _(out=out):
            out[0] = near_other[...]
            out[1] = far_other[...]


def products(left, right):
    slices, rows, _ = left.shape

    def operand(values):
        part = slices // 2
        real = jnp.concatenate([values[i] for i in range(part)], axis=1)
        imag = jnp.concatenate([values[i] for i in range(part, slices)], axis=1)
        return jnp.concatenate([real, imag], axis=0)

    contract = (((1,), (1,)), ((), ()))
    all_parts = lax.dot_general(
        operand(left), operand(right), contract, preferred_element_type=jnp.float32
    )
    scale = 2.0 / (slices * LANES)
    real = all_parts[:rows, :rows] + all_parts[rows:, rows:]
    imag = all_parts[rows:, :rows] - all_parts[:rows, rows:]
    return real * scale, imag * scale


def fill(target, parts, chan_count):
    if len(parts) == 1:
        target[...] = parts[0][...]
        return
    for parity, part in enumerate(parts):
        fill_parity(target, part, chan_count, parity)


def fill_parity(target, part, chan_count, parity):
    own = lax.rem(lax.axis_index("chan"), 2)
    first = own if parity == 0 else 1 - own
    rows = target.shape[2] // chan_count
    for source in range(chan_count // 2):
        span = pl.ds(pl.multiple_of((2 * source + first) * rows, rows), rows)
        target[:, :, span, :] = part[:, :, pl.ds(source * rows, rows), :]


def autos_kernel(chan_count, block_bits, paired, *refs):
    count = 2 if paired else 1
    inputs = refs[: 2 * count]
    block, autos_hbm, autos, sems = refs[-4:]
    half = block.shape[1]
    top = bit_of(lax.axis_index("inp"), block_bits - 1)
    copies = []
    for slot in range(2):
        fill(block.at[slot], inputs[slot * count : (slot + 1) * count], chan_count)
        for group in range(half):
            rows = block[slot, group]
            at = half * (slot * top + (1 - slot) * (1 - top)) + group
            autos[0, slot, group], autos[1, slot, group] = products(rows, rows)
            for part in range(2):
                copy = pltpu.make_async_copy(
                    autos.at[part, slot, group], autos_hbm.at[part, at], sems.at[part, slot, group]
                )
                copy.start()
                copies.append(copy)
    for copy in copies:
        copy.wait()


def autos_call(operands, chan_count, block_bits, after=()):
    half, slices, rows = operands[0].shape[:3]
    paired = len(operands) == 4
    rows *= 2 if paired else 1
    auto_shape = (2, 2, half, rows, rows)
    block_shape = (2, half, slices, rows, LANES)
    return pl.pallas_call(
        functools.partial(autos_kernel, chan_count, block_bits, paired),
        out_shape=[
            jax.ShapeDtypeStruct(block_shape, jnp.bfloat16),
            jax.ShapeDtypeStruct((2, 2 * half, rows, rows), jnp.float32),
        ],
        in_specs=[pl.BlockSpec(memory_space=pltpu.VMEM)] * len(operands)
        + [pl.BlockSpec(memory_space=pl.ANY)] * len(after),
        out_specs=[pl.BlockSpec(memory_space=pltpu.VMEM), pl.BlockSpec(memory_space=pltpu.HBM)],
        scratch_shapes=[
            pltpu.VMEM(auto_shape, jnp.float32),
            pltpu.SemaphoreType.DMA(auto_shape[:3]),
        ],
        compiler_params=pltpu.CompilerParams(vmem_limit_bytes=8 * MIB),
        cost_estimate=pl.CostEstimate(
            flops=16 * half * rows * rows * slices * LANES,
            bytes_accessed=4 << 20,
            transcendentals=0,
        ),
        name="autos",
    )(*operands, *after)


def parts_of(layout, refs):
    found, at = [], 0
    for kind in layout:
        if kind == "stack":
            found.append([refs[at].at[0], refs[at].at[1]])
            at += 1
        else:
            count = 2 if kind == "pair" else 1
            found.append(list(refs[at : at + count]))
            at += count
    return found


def fill_parity_kernel(chan_count, parity, *refs):
    for index, part in enumerate(refs[: -1 - parity]):
        fill_parity(refs[-1].at[index], part, chan_count, parity)


def fill_kernel(*refs):
    for index, part in enumerate(refs[:-1]):
        refs[-1][index] = part[...]


def cross_kernel(chan_count, block_bits, early, late, layout, pairing_hbm, block, filled, *refs):
    inputs, refs = refs[: -len(SCRATCH)], refs[-len(SCRATCH) :]
    vis_hbm, others, vis, pairing_ref, vis_sems, pairing_sem = refs
    pairing_copy = pltpu.make_async_copy(pairing_hbm, pairing_ref, pairing_sem)
    pairing_copy.start()
    own = lax.axis_index("inp")
    top = bit_of(own, block_bits - 1)
    half = block.shape[1]
    for index, parts in enumerate(parts_of(layout, inputs)):
        fill(others.at[index], parts, chan_count)
    partners = [(mask, filled.at[at]) for at, mask in enumerate(early)]
    partners += [(mask, others.at[at]) for at, mask in enumerate(late)]
    copies = []
    for index, (mask, other) in enumerate(partners):
        bit = top_bit(mask)
        slot = 1
        if bit != block_bits - 1:
            slot = (bit_of(own, bit) == top).astype(jnp.int32)
        for group in range(half):
            vis[0, index, group], vis[1, index, group] = products(block[slot, group], other[group])
        if index == 0:
            pairing_copy.wait()
        place = jnp.int32(0)
        for turn_at in range(pairing_ref.shape[0]):
            place = jnp.where(pairing_ref[turn_at] == mask, turn_at, place)
        for part in range(2):
            copy = pltpu.make_async_copy(
                vis.at[part, index], vis_hbm.at[part, place], vis_sems.at[part, index]
            )
            copy.start()
            copies.append(copy)
    for copy in copies:
        copy.wait()


SCRATCH = ("vis_hbm", "others", "vis", "pairing_ref", "vis_sems", "pairing_sem")


def cross_call(pairing, block, received, early, late, chan_count, block_bits):
    _, half, slices, rows, _ = block.shape
    filled_shape = (len(early),) + block.shape[1:]
    cost = functools.partial(pl.CostEstimate, transcendentals=0)
    if received[early[0]][0] == "pair":
        filled = []
        for parity in range(2):
            filled = vmem_call(
                "fill_far" if parity else "fill_near",
                functools.partial(fill_parity_kernel, chan_count, parity),
                [filled_shape],
                [received[mask][1][parity] for mask in early] + list(filled),
                cost=cost(flops=(1 << 29, 4 << 28)[parity], bytes_accessed=(1 << 10, 1 << 20)[parity]),
                aliases={len(early): 0} if parity else None,
            )
    else:
        filled = vmem_call(
            "fill", fill_kernel, [filled_shape], [received[mask][1][0] for mask in early]
        )
    (filled,) = filled
    layout = tuple(received[mask][0] for mask in late)
    operands = [value for mask in late for value in received[mask][1]]
    count = len(early) + len(late)
    vis_shape = (2, count, half, rows, rows)
    return pl.pallas_call(
        functools.partial(cross_kernel, chan_count, block_bits, early, late, layout),
        out_shape=jax.ShapeDtypeStruct(vis_shape, jnp.float32),
        in_specs=[pl.BlockSpec(memory_space=pltpu.HBM)]
        + [pl.BlockSpec(memory_space=pltpu.VMEM)] * (2 + len(operands)),
        out_specs=pl.BlockSpec(memory_space=pltpu.HBM),
        scratch_shapes=[
            pltpu.VMEM((len(late), half, slices, rows, LANES), jnp.bfloat16),
            pltpu.VMEM(vis_shape, jnp.float32),
            pltpu.SMEM(pairing.shape, jnp.int32),
            pltpu.SemaphoreType.DMA(vis_shape[:2]),
            pltpu.SemaphoreType.DMA(()),
        ],
        compiler_params=pltpu.CompilerParams(vmem_limit_bytes=16 * MIB),
        cost_estimate=pl.CostEstimate(
            flops=16 * count * half * rows * rows * slices * LANES,
            bytes_accessed=4 << 20,
            transcendentals=0,
        ),
        name="cross",
    )(pairing, block, filled, *operands)


def on_device(voltages, filter_taps, pairing):
    chan_count = lax.axis_size("chan")
    inp_count = lax.axis_size("inp")
    block_bits = top_bit(inp_count)
    own_chan = lax.axis_index("chan")
    signals = voltages.shape[1]

    def exchange(value, axis, mask):
        count = lax.axis_size(axis)
        return lax.ppermute(value, axis, [(i, i ^ mask) for i in range(count)])

    evens = hops(chan_count)[1:]

    def along(values):
        return [exchange(value, "chan", k) for value, k in zip(values, evens)]

    own_moving, own_other, direct, held, relay_moving, relay_other = spectra_pieces(
        voltages, filter_taps, chan_count
    )
    part = own_moving.shape
    half = part[0]
    relay_moving = exchange(relay_moving, "chan", 1)
    direct = along(direct)
    relay_other = exchange(relay_other, "chan", 1)
    far_own, *onward = vmem_call(
        "split", split_kernel, [part] * (chan_count // 2), [relay_moving], []
    )
    onward = along(onward)
    near, far = [own_moving] + direct, [far_own] + onward
    laid = part[:2] + (chan_count // 2 * signals, LANES)
    whole_tiles = signals % ROWS == 0
    top_mask = inp_count // 2
    if not whole_tiles:
        ordered = np.argsort(hops(chan_count))
        sources = jnp.bitwise_xor(own_chan // 2, jnp.arange(chan_count // 2))

        def merge(parts):
            parts = [parts[at] for at in ordered]
            return jnp.take(jnp.stack(parts, axis=2), sources, axis=2).reshape(laid)

        near, far = [merge(near)], [merge(far)]
    (near,) = vmem_call("near", lay_kernel, [laid], near, [])
    crossed = [exchange(near, "inp", top_mask)]
    (far,) = vmem_call("far", lay_kernel, [laid], far, [])
    crossed.append(exchange(far, "inp", top_mask))
    rest = vmem_call(
        "hand_on",
        hand_on_kernel,
        [(2,) + part] * len(evens),
        [held, relay_other],
        [near],
    )
    rest = along(rest)
    if whole_tiles:
        other_kernel = functools.partial(lay_rest_kernel, len(evens))
        others = [own_other, relay_other] + rest
    else:
        other_kernel = functools.partial(lay_other_kernel, 1)
        others = [
            merge([own_other] + [value[0] for value in rest]),
            merge([relay_other[0]] + [value[1] for value in rest]),
        ]
    near_other, far_other, *sends = vmem_call(
        "other",
        other_kernel,
        [laid] * 2 + [(2,) + laid] * (block_bits - 1),
        [near, far] + others,
        [],
    )
    masks = list(range(1, inp_count))
    received = {top_mask: ("pair", crossed)}
    for mask in masks:
        bit = top_bit(mask)
        if mask == top_mask:
            continue
        if mask > 1 and mask % 2:
            kind, values = received[mask - 1]
            received[mask] = (kind, [exchange(value, "inp", 1) for value in values])
        else:
            kind, values = "pair", [near, far]
            if bit != block_bits - 1:
                kind, values = "stack", [sends[bit]]
            received[mask] = (kind, [exchange(value, "inp", mask) for value in values])
    block = [("pair", [near, far]), ("pair", [near_other, far_other])]
    if not whole_tiles:
        parities = jnp.bitwise_xor(own_chan % 2, jnp.arange(2))

        def interleave(entry):
            kind, values = entry
            if kind == "stack":
                values = [values[0][0], values[0][1]]
            shaped = [value.reshape(half, -1, chan_count // 2, signals, LANES) for value in values]
            ordered = jnp.take(jnp.stack(shaped, axis=3), parities, axis=3)
            return ("whole", [ordered.reshape(half, -1, chan_count * signals, LANES)])

        block = [interleave(entry) for entry in block]
        received = {mask: interleave(entry) for mask, entry in received.items()}
    early = [mask for mask in masks if top_bit(mask) == block_bits - 1]
    late = [mask for mask in masks if top_bit(mask) != block_bits - 1]
    rows, autos = autos_call(
        [value for _, values in block for value in values], chan_count, block_bits, []
    )
    visibilities = cross_call(pairing, rows, received, early, late, chan_count, block_bits)
    return (visibilities, autos)


def solution(mesh):
    in_specs = (P(None, ("inp", "chan"), None), P(), P())
    out_specs = (P(None, None, "chan", "inp", None), P(None, "chan", "inp", None))
    return jax.shard_map(
        on_device, mesh=mesh, in_specs=in_specs, out_specs=out_specs, check_vma=False
    )
```

```python
import functools
import math

import jax
import jax.numpy as jnp
import numpy as np
from jax import lax
from jax.experimental import pallas as pl
from jax.experimental.pallas import tpu as pltpu
from jax.sharding import PartitionSpec as P

AVG = 64
LANES = 128
OUTER = 32
ROWS = 16
MIB = 1024 * 1024


def twiddle_table():
    fine = OUTER * LANES
    k1 = np.arange(OUTER)[None, :, None]
    odd = np.arange(2)[:, None, None]
    q = np.arange(LANES)[None, None, :]
    turned = k1 + OUTER * ((-4 * k1 - 2 * odd) % LANES)
    angle = (turned * q % fine) * (2.0 * math.pi / fine)
    return np.concatenate([np.cos(angle), np.sin(angle)], axis=2).astype(np.float32)


def lane_matrix():
    fine = OUTER * LANES
    q = np.arange(LANES)
    angle = (q[:, None] * q[None, :] % LANES) * (2.0 * math.pi / LANES)
    cos, sin = np.cos(angle), np.sin(angle)
    return (np.block([[cos, -sin], [sin, cos]]) * fine**-0.5).astype(np.float32)


def add(x, y):
    return (x[0] + y[0], x[1] + y[1])


def sub(x, y):
    return (x[0] - y[0], x[1] - y[1])


def minus_i(x):
    return (x[1], -x[0])


def turn(x, step, count):
    step %= count
    if step == 0:
        return x
    if 4 * step == count:
        return minus_i(x)
    if 8 * step == count:
        half = math.sqrt(0.5)
        return ((x[0] + x[1]) * half, (x[1] - x[0]) * half)
    if 8 * step == 3 * count:
        half = math.sqrt(0.5)
        return ((x[1] - x[0]) * half, (x[0] + x[1]) * -half)
    cos, sin = math.cos(2 * math.pi * step / count), math.sin(2 * math.pi * step / count)
    return (x[0] * cos + x[1] * sin, x[1] * cos - x[0] * sin)


def four(x):
    even, odd = add(x[0], x[2]), sub(x[0], x[2])
    other, last = add(x[1], x[3]), minus_i(sub(x[1], x[3]))
    return [add(even, other), add(odd, last), sub(even, other), sub(odd, last)]


def eight(x):
    even, odd = four(x[0::2]), four(x[1::2])
    odd = [turn(value, k, 8) for k, value in enumerate(odd)]
    return [add(e, o) for e, o in zip(even, odd)] + [sub(e, o) for e, o in zip(even, odd)]


def bit_of(value, bit):
    return lax.rem(lax.div(value, 1 << bit), 2)


def top_bit(count):
    return count.bit_length() - 1


def hops(count):
    return [0] + sorted(range(2, count, 2), key=lambda hop: (-top_bit(hop), hop))


def frame_loads(frame_count):
    bounds = [0] + list(range(5, frame_count, 7)) + [frame_count]
    return list(zip(bounds[:-1], bounds[1:]))


def spectra_kernel(chan_count, spectra_count, volt_hbm, taps_hbm, table_hbm, *refs):
    outs, scratch = refs[:-10], refs[-10:]
    volt_ref, taps_ref, table_ref, matrix_ref = scratch[:4]
    filtered, first, last, pieces, volt_sems, table_sems = scratch[4:]
    tap_count, fine = taps_ref.shape
    frame_count = spectra_count + tap_count - 1
    loads = frame_loads(frame_count)
    volt_copies = []
    for at, (begin, end) in enumerate(loads):
        span = pl.ds(begin * fine, (end - begin) * fine)
        volt_copies.append(
            pltpu.make_async_copy(
                volt_hbm.at[:, :, span], volt_ref.at[:, :, span], volt_sems.at[at]
            )
        )
    table_copies = [
        pltpu.make_async_copy(source, target, table_sems.at[at])
        for at, (source, target) in enumerate(
            [(taps_hbm, taps_ref), (table_hbm, table_ref)]
        )
    ]
    volt_copies[0].start()
    table_copies[0].start()
    for copy in volt_copies[1:]:
        copy.start()
    table_copies[1].start()
    for at, (begin, end) in enumerate(loads):
        if at == 0:
            table_copies[0].wait()
        volt_copies[at].wait()

        def filter_column(p, carry, begin=begin, end=end):
            column = pl.multiple_of(p * LANES, LANES)
            taps = {}
            for t in range(max(0, begin - spectra_count + 1), min(tap_count, end)):
                taps[t] = taps_ref[pl.ds(t, 1), pl.ds(column, LANES)]
            for part in range(2):
                sums = {}
                for frame in range(begin, end):
                    lane = pl.multiple_of(frame * fine + column, LANES)
                    values = volt_ref[part, :, pl.ds(lane, LANES)].astype(jnp.float32)
                    for s in range(spectra_count):
                        if 0 <= frame - s < tap_count:
                            term = taps[frame - s] * values
                            if s not in sums and frame > s:
                                sums[s] = filtered[s, part, p]
                            sums[s] = sums[s] + term if s in sums else term
                for s, total in sums.items():
                    filtered[s, part, p] = total
            return carry

        lax.fori_loop(0, OUTER, filter_column, 0, unroll=4)
    table_copies[1].wait()
    table = table_ref[pl.ds(0, 2 * LANES), :]
    matrix_ref[0] = table.astype(jnp.bfloat16)
    matrix_ref[1] = (table - matrix_ref[0].astype(jnp.float32)).astype(jnp.bfloat16)

    def transform(s, carry):
        for a in range(8):
            values = four([(filtered[s, 0, a + 8 * b], filtered[s, 1, a + 8 * b]) for b in range(4)])
            for r in range(4):
                real, imag = turn(values[r], a * r, OUTER)
                first[0, r, a] = real
                first[1, r, a] = imag
        odd = s % 2
        for r in range(4):
            values = eight([(first[0, r, a], first[1, r, a]) for a in range(8)])
            highs, lows = [], []
            for t in range(8):
                k1 = r + 4 * t
                factors = table_ref[pl.ds(2 * LANES + odd * OUTER + k1, 1), :]
                cos, sin = factors[:, :LANES], factors[:, LANES:]
                real, imag = values[t]
                row = jnp.concatenate([real * cos + imag * sin, imag * cos - real * sin], axis=1)
                high = row.astype(jnp.bfloat16)
                highs.append(high)
                lows.append((row - high.astype(jnp.float32)).astype(jnp.bfloat16))
            high = jnp.concatenate(highs, axis=0)
            low = jnp.concatenate(lows, axis=0)
            dot = functools.partial(jnp.dot, preferred_element_type=jnp.float32)
            result = dot(high, matrix_ref[0]) + (dot(low, matrix_ref[0]) + dot(high, matrix_ref[1]))
            result = result.astype(jnp.bfloat16)
            for t in range(8):
                rows = result[t * ROWS : (t + 1) * ROWS]
                last[s, 0, r + 4 * t] = rows[:, :LANES]
                last[s, 1, r + 4 * t] = rows[:, LANES:]
        return carry


    lane = lax.broadcasted_iota(jnp.int32, (ROWS, LANES), 1)
    bits = [(lane >> bit) & 1 == 1 for bit in range(7)]
    group_count = pieces.shape[1]

    def regroup(part, pair):
        even = [last[2 * pair, part, k1] for k1 in range(OUTER)]
        odd = [last[2 * pair + 1, part, k1] for k1 in range(OUTER)]
        mixed = [
            [jnp.where(bits[1], odd[v], even[v]) for v in range(OUTER)],
            [jnp.where(bits[1], even[v], odd[v - 1]) for v in range(OUTER)],
        ]
        for which in range(2):
            tiles = [mixed[which][-v % OUTER] for v in range(OUTER)]
            for bit in range(5):
                tiles = [
                    jnp.where(bits[2 + bit], tiles[v - (1 << bit)], tiles[v])
                    for v in range(OUTER)
                ]
            for u in range(OUTER):
                chan, group = divmod(2 * u + which, group_count)
                pieces[chan, group, part * (spectra_count // 2) + pair] = tiles[u]

    for s in range(spectra_count):
        transform(s, 0)
        if s % 2:
            regroup(0, s // 2)
            regroup(1, s // 2)

    own = lax.axis_index("chan")
    top = bit_of(lax.axis_index("inp"), top_bit(lax.axis_size("inp")) - 1)
    half = group_count // 2
    moving, other = pl.ds((1 - top) * half, half), pl.ds(top * half, half)
    own_moving, own_other, *direct, held, relay_moving, relay_other = outs
    own_moving[...] = pieces[own, moving]
    own_other[...] = pieces[own, other]
    for index, hop in enumerate(hops(chan_count)):
        chan = jnp.bitwise_xor(own, hop)
        if index:
            direct[index - 1][...] = pieces[chan, moving]
            held[index - 1] = pieces[chan, other]
        relay_moving[index] = pieces[jnp.bitwise_xor(chan, 1), moving]
        relay_other[index] = pieces[jnp.bitwise_xor(chan, 1), other]


def spectra_pieces(voltages, filter_taps, chan_count):
    tap_count, fine = filter_taps.shape
    signals = voltages.shape[1]
    spectra_count = voltages.shape[2] // fine - tap_count + 1
    padded = -signals % ROWS
    if padded:
        voltages = jnp.pad(voltages, ((0, 0), (0, padded), (0, 0)))
    group_count = fine // AVG // chan_count
    slices = spectra_count
    piece = (group_count, slices, ROWS, LANES)
    part = (group_count // 2, slices, ROWS, LANES)
    half_count = chan_count // 2
    shapes = [part] * (half_count + 1) + [(half_count - 1,) + part] + [(half_count,) + part] * 2
    table = np.concatenate([lane_matrix(), twiddle_table().reshape(-1, 2 * LANES)])
    outs = pl.pallas_call(
        functools.partial(spectra_kernel, chan_count, spectra_count),
        out_shape=[jax.ShapeDtypeStruct(shape, jnp.bfloat16) for shape in shapes],
        in_specs=[pl.BlockSpec(memory_space=pltpu.HBM)] * 3,
        out_specs=[pl.BlockSpec(memory_space=pltpu.VMEM)] * len(shapes),
        scratch_shapes=[
            pltpu.VMEM(voltages.shape, jnp.bfloat16),
            pltpu.VMEM(filter_taps.shape, jnp.float32),
            pltpu.VMEM(table.shape, jnp.float32),
            pltpu.VMEM((2, 2 * LANES, 2 * LANES), jnp.bfloat16),
            pltpu.VMEM((spectra_count, 2, OUTER, ROWS, LANES), jnp.float32),
            pltpu.VMEM((2, 4, 8, ROWS, LANES), jnp.float32),
            pltpu.VMEM((spectra_count, 2, OUTER, ROWS, LANES), jnp.bfloat16),
            pltpu.VMEM((chan_count,) + piece, jnp.bfloat16),
            pltpu.SemaphoreType.DMA((len(frame_loads(spectra_count + tap_count - 1)),)),
            pltpu.SemaphoreType.DMA((2,)),
        ],
        compiler_params=pltpu.CompilerParams(vmem_limit_bytes=53 * MIB),
        name="spectra",
    )(voltages, filter_taps, jnp.asarray(table))
    outs = [out[..., :signals, :] for out in outs]
    return outs[:2] + [outs[2:-3]] + outs[-3:]


def vmem_call(name, kernel, out_shapes, operands, after=(), cost=None, aliases=None):
    count = len(operands)
    operands = list(operands) + list(after)

    def body(*refs):
        kernel(*refs[:count], *refs[len(operands) :])

    return pl.pallas_call(
        body,
        out_shape=[jax.ShapeDtypeStruct(shape, jnp.bfloat16) for shape in out_shapes],
        in_specs=[pl.BlockSpec(memory_space=pltpu.VMEM)] * count
        + [pl.BlockSpec(memory_space=pl.ANY)] * len(after),
        out_specs=[pl.BlockSpec(memory_space=pltpu.VMEM)] * len(out_shapes),
        compiler_params=pltpu.CompilerParams(vmem_limit_bytes=8 * MIB),
        cost_estimate=cost,
        input_output_aliases=aliases or {},
        name=name,
    )(*operands)


def split_kernel(relayed, *outs):
    for index, out in enumerate(outs):
        out[...] = relayed[index]


def hand_on_kernel(held, relayed, *outs):
    for index, out in enumerate(outs):
        out[0] = held[index]
        out[1] = relayed[index + 1]


def lay(out, pieces):
    count = len(pieces)
    if count == 1:
        out[...] = pieces[0][...]
        return
    own = lax.axis_index("chan")
    rows = out.shape[2] // count
    for hop, piece in zip(hops(2 * count), pieces):
        source = lax.div(jnp.bitwise_xor(own, hop), 2)
        span = pl.ds(pl.multiple_of(source * rows, rows), rows)
        out[:, :, span, :] = piece[...]


def lay_kernel(*refs):
    lay(refs[-1], refs[:-1])


def lay_rest_kernel(rest_count, near_moving, far_moving, own_other, relayed, *refs):
    rest, outs = refs[:rest_count], refs[rest_count:]
    near = [own_other] + [value.at[0] for value in rest]
    far = [relayed.at[0]] + [value.at[1] for value in rest]
    lay_other_kernel(len(near), near_moving, far_moving, *near, *far, *outs)


def lay_other_kernel(piece_count, near_moving, far_moving, *refs):
    near, far = refs[:piece_count], refs[piece_count : 2 * piece_count]
    near_other, far_other, *sends = refs[2 * piece_count :]
    lay(near_other, near)
    lay(far_other, far)
    block = lax.axis_index("inp")
    top = bit_of(block, len(sends))
    for bit, out in enumerate(sends):
        same = bit_of(block, bit) == top

        @pl.when(same)
        def _(out=out):
            out[0] = near_moving[...]
            out[1] = far_moving[...]

        @pl.when(jnp.logical_not(same))
        def _(out=out):
            out[0] = near_other[...]
            out[1] = far_other[...]


def products(left, right):
    slices, rows, _ = left.shape

    def operand(values):
        part = slices // 2
        real = jnp.concatenate([values[i] for i in range(part)], axis=1)
        imag = jnp.concatenate([values[i] for i in range(part, slices)], axis=1)
        return jnp.concatenate([real, imag], axis=0)

    contract = (((1,), (1,)), ((), ()))
    all_parts = lax.dot_general(
        operand(left), operand(right), contract, preferred_element_type=jnp.float32
    )
    scale = 2.0 / (slices * LANES)
    real = all_parts[:rows, :rows] + all_parts[rows:, rows:]
    imag = all_parts[rows:, :rows] - all_parts[:rows, rows:]
    return real * scale, imag * scale


def fill(target, parts, chan_count):
    if len(parts) == 1:
        target[...] = parts[0][...]
        return
    for parity, part in enumerate(parts):
        fill_parity(target, part, chan_count, parity)


def fill_parity(target, part, chan_count, parity):
    own = lax.rem(lax.axis_index("chan"), 2)
    first = own if parity == 0 else 1 - own
    rows = target.shape[2] // chan_count
    for source in range(chan_count // 2):
        span = pl.ds(pl.multiple_of((2 * source + first) * rows, rows), rows)
        target[:, :, span, :] = part[:, :, pl.ds(source * rows, rows), :]


def autos_kernel(chan_count, block_bits, paired, *refs):
    count = 2 if paired else 1
    inputs = refs[: 2 * count]
    block, autos_hbm, autos, sems = refs[-4:]
    half = block.shape[1]
    top = bit_of(lax.axis_index("inp"), block_bits - 1)
    copies = []
    for slot in range(2):
        fill(block.at[slot], inputs[slot * count : (slot + 1) * count], chan_count)
        for group in range(half):
            rows = block[slot, group]
            at = half * (slot * top + (1 - slot) * (1 - top)) + group
            autos[0, slot, group], autos[1, slot, group] = products(rows, rows)
            for part in range(2):
                copy = pltpu.make_async_copy(
                    autos.at[part, slot, group], autos_hbm.at[part, at], sems.at[part, slot, group]
                )
                copy.start()
                copies.append(copy)
    for copy in copies:
        copy.wait()


def autos_call(operands, chan_count, block_bits, after=()):
    half, slices, rows = operands[0].shape[:3]
    paired = len(operands) == 4
    rows *= 2 if paired else 1
    auto_shape = (2, 2, half, rows, rows)
    block_shape = (2, half, slices, rows, LANES)
    return pl.pallas_call(
        functools.partial(autos_kernel, chan_count, block_bits, paired),
        out_shape=[
            jax.ShapeDtypeStruct(block_shape, jnp.bfloat16),
            jax.ShapeDtypeStruct((2, 2 * half, rows, rows), jnp.float32),
        ],
        in_specs=[pl.BlockSpec(memory_space=pltpu.VMEM)] * len(operands)
        + [pl.BlockSpec(memory_space=pl.ANY)] * len(after),
        out_specs=[pl.BlockSpec(memory_space=pltpu.VMEM), pl.BlockSpec(memory_space=pltpu.HBM)],
        scratch_shapes=[
            pltpu.VMEM(auto_shape, jnp.float32),
            pltpu.SemaphoreType.DMA(auto_shape[:3]),
        ],
        compiler_params=pltpu.CompilerParams(vmem_limit_bytes=8 * MIB),
        cost_estimate=pl.CostEstimate(
            flops=16 * half * rows * rows * slices * LANES,
            bytes_accessed=4 << 20,
            transcendentals=0,
        ),
        name="autos",
    )(*operands, *after)


def parts_of(layout, refs):
    found, at = [], 0
    for kind in layout:
        if kind == "stack":
            found.append([refs[at].at[0], refs[at].at[1]])
            at += 1
        else:
            count = 2 if kind == "pair" else 1
            found.append(list(refs[at : at + count]))
            at += count
    return found


def fill_parity_kernel(chan_count, parity, *refs):
    for index, part in enumerate(refs[: -1 - parity]):
        fill_parity(refs[-1].at[index], part, chan_count, parity)


def fill_kernel(*refs):
    for index, part in enumerate(refs[:-1]):
        refs[-1][index] = part[...]


def cross_kernel(chan_count, block_bits, early, late, layout, pairing_hbm, block, filled, *refs):
    inputs, refs = refs[: -len(SCRATCH)], refs[-len(SCRATCH) :]
    vis_hbm, others, vis, pairing_ref, vis_sems, pairing_sem = refs
    pairing_copy = pltpu.make_async_copy(pairing_hbm, pairing_ref, pairing_sem)
    pairing_copy.start()
    own = lax.axis_index("inp")
    top = bit_of(own, block_bits - 1)
    half = block.shape[1]
    for index, parts in enumerate(parts_of(layout, inputs)):
        fill(others.at[index], parts, chan_count)
    partners = [(mask, filled.at[at]) for at, mask in enumerate(early)]
    partners += [(mask, others.at[at]) for at, mask in enumerate(late)]
    copies = []
    for index, (mask, other) in enumerate(partners):
        bit = top_bit(mask)
        slot = 1
        if bit != block_bits - 1:
            slot = (bit_of(own, bit) == top).astype(jnp.int32)
        for group in range(half):
            vis[0, index, group], vis[1, index, group] = products(block[slot, group], other[group])
        if index == 0:
            pairing_copy.wait()
        place = jnp.int32(0)
        for turn_at in range(pairing_ref.shape[0]):
            place = jnp.where(pairing_ref[turn_at] == mask, turn_at, place)
        for part in range(2):
            copy = pltpu.make_async_copy(
                vis.at[part, index], vis_hbm.at[part, place], vis_sems.at[part, index]
            )
            copy.start()
            copies.append(copy)
    for copy in copies:
        copy.wait()


SCRATCH = ("vis_hbm", "others", "vis", "pairing_ref", "vis_sems", "pairing_sem")


def cross_call(pairing, block, received, early, late, chan_count, block_bits):
    _, half, slices, rows, _ = block.shape
    filled_shape = (len(early),) + block.shape[1:]
    cost = functools.partial(pl.CostEstimate, transcendentals=0)
    if received[early[0]][0] == "pair":
        filled = []
        for parity in range(2):
            filled = vmem_call(
                "fill_far" if parity else "fill_near",
                functools.partial(fill_parity_kernel, chan_count, parity),
                [filled_shape],
                [received[mask][1][parity] for mask in early] + list(filled),
                cost=cost(flops=(1 << 29, 4 << 28)[parity], bytes_accessed=(1 << 10, 1 << 20)[parity]),
                aliases={len(early): 0} if parity else None,
            )
    else:
        filled = vmem_call(
            "fill", fill_kernel, [filled_shape], [received[mask][1][0] for mask in early]
        )
    (filled,) = filled
    layout = tuple(received[mask][0] for mask in late)
    operands = [value for mask in late for value in received[mask][1]]
    count = len(early) + len(late)
    vis_shape = (2, count, half, rows, rows)
    return pl.pallas_call(
        functools.partial(cross_kernel, chan_count, block_bits, early, late, layout),
        out_shape=jax.ShapeDtypeStruct(vis_shape, jnp.float32),
        in_specs=[pl.BlockSpec(memory_space=pltpu.HBM)]
        + [pl.BlockSpec(memory_space=pltpu.VMEM)] * (2 + len(operands)),
        out_specs=pl.BlockSpec(memory_space=pltpu.HBM),
        scratch_shapes=[
            pltpu.VMEM((len(late), half, slices, rows, LANES), jnp.bfloat16),
            pltpu.VMEM(vis_shape, jnp.float32),
            pltpu.SMEM(pairing.shape, jnp.int32),
            pltpu.SemaphoreType.DMA(vis_shape[:2]),
            pltpu.SemaphoreType.DMA(()),
        ],
        compiler_params=pltpu.CompilerParams(vmem_limit_bytes=16 * MIB),
        cost_estimate=pl.CostEstimate(
            flops=16 * count * half * rows * rows * slices * LANES,
            bytes_accessed=4 << 20,
            transcendentals=0,
        ),
        name="cross",
    )(pairing, block, filled, *operands)


def on_device(voltages, filter_taps, pairing):
    chan_count = lax.axis_size("chan")
    inp_count = lax.axis_size("inp")
    block_bits = top_bit(inp_count)
    own_chan = lax.axis_index("chan")
    signals = voltages.shape[1]

    def exchange(value, axis, mask):
        count = lax.axis_size(axis)
        return lax.ppermute(value, axis, [(i, i ^ mask) for i in range(count)])

    evens = hops(chan_count)[1:]

    def along(values):
        return [exchange(value, "chan", k) for value, k in zip(values, evens)]

    own_moving, own_other, direct, held, relay_moving, relay_other = spectra_pieces(
        voltages, filter_taps, chan_count
    )
    part = own_moving.shape
    half = part[0]
    relay_moving = exchange(relay_moving, "chan", 1)
    direct = along(direct)
    relay_other = exchange(relay_other, "chan", 1)
    far_own, *onward = vmem_call(
        "split", split_kernel, [part] * (chan_count // 2), [relay_moving], []
    )
    onward = along(onward)
    near, far = [own_moving] + direct, [far_own] + onward
    laid = part[:2] + (chan_count // 2 * signals, LANES)
    whole_tiles = signals % ROWS == 0
    top_mask = inp_count // 2
    if not whole_tiles:
        ordered = np.argsort(hops(chan_count))
        sources = jnp.bitwise_xor(own_chan // 2, jnp.arange(chan_count // 2))

        def merge(parts):
            parts = [parts[at] for at in ordered]
            return jnp.take(jnp.stack(parts, axis=2), sources, axis=2).reshape(laid)

        near, far = [merge(near)], [merge(far)]
    (near,) = vmem_call("near", lay_kernel, [laid], near, [])
    crossed = [exchange(near, "inp", top_mask)]
    (far,) = vmem_call("far", lay_kernel, [laid], far, [])
    crossed.append(exchange(far, "inp", top_mask))
    rest = vmem_call(
        "hand_on",
        hand_on_kernel,
        [(2,) + part] * len(evens),
        [held, relay_other],
        [near],
    )
    rest = along(rest)
    if whole_tiles:
        other_kernel = functools.partial(lay_rest_kernel, len(evens))
        others = [own_other, relay_other] + rest
    else:
        other_kernel = functools.partial(lay_other_kernel, 1)
        others = [
            merge([own_other] + [value[0] for value in rest]),
            merge([relay_other[0]] + [value[1] for value in rest]),
        ]
    near_other, far_other, *sends = vmem_call(
        "other",
        other_kernel,
        [laid] * 2 + [(2,) + laid] * (block_bits - 1),
        [near, far] + others,
        [],
    )
    masks = list(range(1, inp_count))
    received = {top_mask: ("pair", crossed)}
    for mask in masks:
        bit = top_bit(mask)
        if mask == top_mask:
            continue
        if mask > 1 and mask % 2:
            kind, values = received[mask - 1]
            received[mask] = (kind, [exchange(value, "inp", 1) for value in values])
        else:
            kind, values = "pair", [near, far]
            if bit != block_bits - 1:
                kind, values = "stack", [sends[bit]]
            received[mask] = (kind, [exchange(value, "inp", mask) for value in values])
    block = [("pair", [near, far]), ("pair", [near_other, far_other])]
    if not whole_tiles:
        parities = jnp.bitwise_xor(own_chan % 2, jnp.arange(2))

        def interleave(entry):
            kind, values = entry
            if kind == "stack":
                values = [values[0][0], values[0][1]]
            shaped = [value.reshape(half, -1, chan_count // 2, signals, LANES) for value in values]
            ordered = jnp.take(jnp.stack(shaped, axis=3), parities, axis=3)
            return ("whole", [ordered.reshape(half, -1, chan_count * signals, LANES)])

        block = [interleave(entry) for entry in block]
        received = {mask: interleave(entry) for mask, entry in received.items()}
    early = [mask for mask in masks if top_bit(mask) == block_bits - 1]
    late = [mask for mask in masks if top_bit(mask) != block_bits - 1]
    rows, autos = autos_call(
        [value for _, values in block for value in values], chan_count, block_bits, []
    )
    visibilities = cross_call(pairing, rows, received, early, late, chan_count, block_bits)
    return (visibilities, autos)


def solution(mesh):
    in_specs = (P(None, ("inp", "chan"), None), P(), P())
    out_specs = (P(None, None, "chan", "inp", None), P(None, "chan", "inp", None))
    return jax.shard_map(
        on_device, mesh=mesh, in_specs=in_specs, out_specs=out_specs, check_vma=False
    )
```

```python
import functools
import math

import jax
import jax.numpy as jnp
import numpy as np
from jax import lax
from jax.experimental import pallas as pl
from jax.experimental.pallas import tpu as pltpu
from jax.sharding import PartitionSpec as P

AVG = 64
LANES = 128
OUTER = 32
ROWS = 16
MIB = 1024 * 1024
FILL_FLOPS = (9 << 26, 9 << 27)


def twiddle_table():
    fine = OUTER * LANES
    k1 = np.arange(OUTER)[None, :, None]
    odd = np.arange(2)[:, None, None]
    q = np.arange(LANES)[None, None, :]
    turned = k1 + OUTER * ((-4 * k1 - 2 * odd) % LANES)
    angle = (turned * q % fine) * (2.0 * math.pi / fine)
    return np.concatenate([np.cos(angle), np.sin(angle)], axis=2).astype(np.float32)


def lane_matrix():
    fine = OUTER * LANES
    q = np.arange(LANES)
    angle = (q[:, None] * q[None, :] % LANES) * (2.0 * math.pi / LANES)
    cos, sin = np.cos(angle), np.sin(angle)
    return (np.block([[cos, -sin], [sin, cos]]) * fine**-0.5).astype(np.float32)


def add(x, y):
    return (x[0] + y[0], x[1] + y[1])


def sub(x, y):
    return (x[0] - y[0], x[1] - y[1])


def minus_i(x):
    return (x[1], -x[0])


def turn(x, step, count):
    step %= count
    if step == 0:
        return x
    if 4 * step == count:
        return minus_i(x)
    if 8 * step == count:
        half = math.sqrt(0.5)
        return ((x[0] + x[1]) * half, (x[1] - x[0]) * half)
    if 8 * step == 3 * count:
        half = math.sqrt(0.5)
        return ((x[1] - x[0]) * half, (x[0] + x[1]) * -half)
    cos, sin = math.cos(2 * math.pi * step / count), math.sin(2 * math.pi * step / count)
    return (x[0] * cos + x[1] * sin, x[1] * cos - x[0] * sin)


def four(x):
    even, odd = add(x[0], x[2]), sub(x[0], x[2])
    other, last = add(x[1], x[3]), minus_i(sub(x[1], x[3]))
    return [add(even, other), add(odd, last), sub(even, other), sub(odd, last)]


def eight(x):
    even, odd = four(x[0::2]), four(x[1::2])
    odd = [turn(value, k, 8) for k, value in enumerate(odd)]
    return [add(e, o) for e, o in zip(even, odd)] + [sub(e, o) for e, o in zip(even, odd)]


def bit_of(value, bit):
    return lax.rem(lax.div(value, 1 << bit), 2)


def top_bit(count):
    return count.bit_length() - 1


def hops(count):
    return [0] + sorted(range(2, count, 2), key=lambda hop: (-top_bit(hop), hop))


def frame_loads(frame_count):
    bounds = [0] + list(range(5, frame_count, 7)) + [frame_count]
    return list(zip(bounds[:-1], bounds[1:]))


def spectra_kernel(chan_count, spectra_count, volt_hbm, taps_hbm, table_hbm, *refs):
    outs, scratch = refs[:-10], refs[-10:]
    volt_ref, taps_ref, table_ref, matrix_ref = scratch[:4]
    filtered, first, last, pieces, volt_sems, table_sems = scratch[4:]
    tap_count, fine = taps_ref.shape
    frame_count = spectra_count + tap_count - 1
    loads = frame_loads(frame_count)
    volt_copies = []
    for at, (begin, end) in enumerate(loads):
        span = pl.ds(begin * fine, (end - begin) * fine)
        volt_copies.append(
            pltpu.make_async_copy(
                volt_hbm.at[:, :, span], volt_ref.at[:, :, span], volt_sems.at[at]
            )
        )
    table_copies = [
        pltpu.make_async_copy(source, target, table_sems.at[at])
        for at, (source, target) in enumerate(
            [(taps_hbm, taps_ref), (table_hbm, table_ref)]
        )
    ]
    volt_copies[0].start()
    table_copies[0].start()
    for copy in volt_copies[1:]:
        copy.start()
    table_copies[1].start()
    for at, (begin, end) in enumerate(loads):
        if at == 0:
            table_copies[0].wait()
        volt_copies[at].wait()

        def filter_column(p, carry, begin=begin, end=end):
            column = pl.multiple_of(p * LANES, LANES)
            taps = {}
            for t in range(max(0, begin - spectra_count + 1), min(tap_count, end)):
                taps[t] = taps_ref[pl.ds(t, 1), pl.ds(column, LANES)]
            for part in range(2):
                sums = {}
                for frame in range(begin, end):
                    lane = pl.multiple_of(frame * fine + column, LANES)
                    values = volt_ref[part, :, pl.ds(lane, LANES)].astype(jnp.float32)
                    for s in range(spectra_count):
                        if 0 <= frame - s < tap_count:
                            term = taps[frame - s] * values
                            if s not in sums and frame > s:
                                sums[s] = filtered[s, part, p]
                            sums[s] = sums[s] + term if s in sums else term
                for s, total in sums.items():
                    filtered[s, part, p] = total
            return carry

        lax.fori_loop(0, OUTER, filter_column, 0, unroll=4)
    table_copies[1].wait()
    table = table_ref[pl.ds(0, 2 * LANES), :]
    matrix_ref[0] = table.astype(jnp.bfloat16)
    matrix_ref[1] = (table - matrix_ref[0].astype(jnp.float32)).astype(jnp.bfloat16)

    def transform(s, carry):
        for a in range(8):
            values = four([(filtered[s, 0, a + 8 * b], filtered[s, 1, a + 8 * b]) for b in range(4)])
            for r in range(4):
                real, imag = turn(values[r], a * r, OUTER)
                first[0, r, a] = real
                first[1, r, a] = imag
        odd = s % 2
        for r in range(4):
            values = eight([(first[0, r, a], first[1, r, a]) for a in range(8)])
            highs, lows = [], []
            for t in range(8):
                k1 = r + 4 * t
                factors = table_ref[pl.ds(2 * LANES + odd * OUTER + k1, 1), :]
                cos, sin = factors[:, :LANES], factors[:, LANES:]
                real, imag = values[t]
                row = jnp.concatenate([real * cos + imag * sin, imag * cos - real * sin], axis=1)
                high = row.astype(jnp.bfloat16)
                highs.append(high)
                lows.append((row - high.astype(jnp.float32)).astype(jnp.bfloat16))
            high = jnp.concatenate(highs, axis=0)
            low = jnp.concatenate(lows, axis=0)
            dot = functools.partial(jnp.dot, preferred_element_type=jnp.float32)
            result = dot(high, matrix_ref[0]) + (dot(low, matrix_ref[0]) + dot(high, matrix_ref[1]))
            result = result.astype(jnp.bfloat16)
            for t in range(8):
                rows = result[t * ROWS : (t + 1) * ROWS]
                last[s, 0, r + 4 * t] = rows[:, :LANES]
                last[s, 1, r + 4 * t] = rows[:, LANES:]
        return carry


    lane = lax.broadcasted_iota(jnp.int32, (ROWS, LANES), 1)
    bits = [(lane >> bit) & 1 == 1 for bit in range(7)]
    group_count = pieces.shape[1]

    def regroup(part, pair):
        even = [last[2 * pair, part, k1] for k1 in range(OUTER)]
        odd = [last[2 * pair + 1, part, k1] for k1 in range(OUTER)]
        mixed = [
            [jnp.where(bits[1], odd[v], even[v]) for v in range(OUTER)],
            [jnp.where(bits[1], even[v], odd[v - 1]) for v in range(OUTER)],
        ]
        for which in range(2):
            tiles = [mixed[which][-v % OUTER] for v in range(OUTER)]
            for bit in range(5):
                tiles = [
                    jnp.where(bits[2 + bit], tiles[v - (1 << bit)], tiles[v])
                    for v in range(OUTER)
                ]
            for u in range(OUTER):
                chan, group = divmod(2 * u + which, group_count)
                pieces[chan, group, part * (spectra_count // 2) + pair] = tiles[u]

    for s in range(spectra_count):
        transform(s, 0)
        if s % 2:
            regroup(0, s // 2)
            regroup(1, s // 2)

    own = lax.axis_index("chan")
    top = bit_of(lax.axis_index("inp"), top_bit(lax.axis_size("inp")) - 1)
    half = group_count // 2
    moving, other = pl.ds((1 - top) * half, half), pl.ds(top * half, half)
    own_moving, own_other, *direct, held, relay_moving, relay_other = outs
    own_moving[...] = pieces[own, moving]
    own_other[...] = pieces[own, other]
    for index, hop in enumerate(hops(chan_count)):
        chan = jnp.bitwise_xor(own, hop)
        if index:
            direct[index - 1][...] = pieces[chan, moving]
            held[index - 1] = pieces[chan, other]
        relay_moving[index] = pieces[jnp.bitwise_xor(chan, 1), moving]
        relay_other[index] = pieces[jnp.bitwise_xor(chan, 1), other]


def spectra_pieces(voltages, filter_taps, chan_count):
    tap_count, fine = filter_taps.shape
    signals = voltages.shape[1]
    spectra_count = voltages.shape[2] // fine - tap_count + 1
    padded = -signals % ROWS
    if padded:
        voltages = jnp.pad(voltages, ((0, 0), (0, padded), (0, 0)))
    group_count = fine // AVG // chan_count
    slices = spectra_count
    piece = (group_count, slices, ROWS, LANES)
    part = (group_count // 2, slices, ROWS, LANES)
    half_count = chan_count // 2
    shapes = [part] * (half_count + 1) + [(half_count - 1,) + part] + [(half_count,) + part] * 2
    table = np.concatenate([lane_matrix(), twiddle_table().reshape(-1, 2 * LANES)])
    outs = pl.pallas_call(
        functools.partial(spectra_kernel, chan_count, spectra_count),
        out_shape=[jax.ShapeDtypeStruct(shape, jnp.bfloat16) for shape in shapes],
        in_specs=[pl.BlockSpec(memory_space=pltpu.HBM)] * 3,
        out_specs=[pl.BlockSpec(memory_space=pltpu.VMEM)] * len(shapes),
        scratch_shapes=[
            pltpu.VMEM(voltages.shape, jnp.bfloat16),
            pltpu.VMEM(filter_taps.shape, jnp.float32),
            pltpu.VMEM(table.shape, jnp.float32),
            pltpu.VMEM((2, 2 * LANES, 2 * LANES), jnp.bfloat16),
            pltpu.VMEM((spectra_count, 2, OUTER, ROWS, LANES), jnp.float32),
            pltpu.VMEM((2, 4, 8, ROWS, LANES), jnp.float32),
            pltpu.VMEM((spectra_count, 2, OUTER, ROWS, LANES), jnp.bfloat16),
            pltpu.VMEM((chan_count,) + piece, jnp.bfloat16),
            pltpu.SemaphoreType.DMA((len(frame_loads(spectra_count + tap_count - 1)),)),
            pltpu.SemaphoreType.DMA((2,)),
        ],
        compiler_params=pltpu.CompilerParams(vmem_limit_bytes=53 * MIB),
        name="spectra",
    )(voltages, filter_taps, jnp.asarray(table))
    outs = [out[..., :signals, :] for out in outs]
    return outs[:2] + [outs[2:-3]] + outs[-3:]


def vmem_call(name, kernel, out_shapes, operands, after=(), cost=None, aliases=None):
    count = len(operands)
    operands = list(operands) + list(after)

    def body(*refs):
        kernel(*refs[:count], *refs[len(operands) :])

    return pl.pallas_call(
        body,
        out_shape=[jax.ShapeDtypeStruct(shape, jnp.bfloat16) for shape in out_shapes],
        in_specs=[pl.BlockSpec(memory_space=pltpu.VMEM)] * count
        + [pl.BlockSpec(memory_space=pl.ANY)] * len(after),
        out_specs=[pl.BlockSpec(memory_space=pltpu.VMEM)] * len(out_shapes),
        compiler_params=pltpu.CompilerParams(vmem_limit_bytes=8 * MIB),
        cost_estimate=cost,
        input_output_aliases=aliases or {},
        name=name,
    )(*operands)


def split_kernel(relayed, *outs):
    for index, out in enumerate(outs):
        out[...] = relayed[index]


def hand_on_kernel(held, relayed, *outs):
    for index, out in enumerate(outs):
        out[0] = held[index]
        out[1] = relayed[index + 1]


def lay(out, pieces):
    count = len(pieces)
    if count == 1:
        out[...] = pieces[0][...]
        return
    own = lax.axis_index("chan")
    rows = out.shape[2] // count
    for hop, piece in zip(hops(2 * count), pieces):
        source = lax.div(jnp.bitwise_xor(own, hop), 2)
        span = pl.ds(pl.multiple_of(source * rows, rows), rows)
        out[:, :, span, :] = piece[...]


def lay_kernel(*refs):
    lay(refs[-1], refs[:-1])


def lay_rest_kernel(rest_count, near_moving, far_moving, own_other, relayed, *refs):
    rest, outs = refs[:rest_count], refs[rest_count:]
    near = [own_other] + [value.at[0] for value in rest]
    far = [relayed.at[0]] + [value.at[1] for value in rest]
    lay_other_kernel(len(near), near_moving, far_moving, *near, *far, *outs)


def lay_other_kernel(piece_count, near_moving, far_moving, *refs):
    near, far = refs[:piece_count], refs[piece_count : 2 * piece_count]
    near_other, far_other, *sends = refs[2 * piece_count :]
    lay(near_other, near)
    lay(far_other, far)
    block = lax.axis_index("inp")
    top = bit_of(block, len(sends))
    for bit, out in enumerate(sends):
        same = bit_of(block, bit) == top

        @pl.when(same)
        def _(out=out):
            out[0] = near_moving[...]
            out[1] = far_moving[...]

        @pl.when(jnp.logical_not(same))
        def _(out=out):
            out[0] = near_other[...]
            out[1] = far_other[...]


def products(left, right):
    slices, rows, _ = left.shape

    def operand(values):
        part = slices // 2
        real = jnp.concatenate([values[i] for i in range(part)], axis=1)
        imag = jnp.concatenate([values[i] for i in range(part, slices)], axis=1)
        return jnp.concatenate([real, imag], axis=0)

    contract = (((1,), (1,)), ((), ()))
    all_parts = lax.dot_general(
        operand(left), operand(right), contract, preferred_element_type=jnp.float32
    )
    scale = 2.0 / (slices * LANES)
    real = all_parts[:rows, :rows] + all_parts[rows:, rows:]
    imag = all_parts[rows:, :rows] - all_parts[:rows, rows:]
    return real * scale, imag * scale


def fill(target, parts, chan_count):
    if len(parts) == 1:
        target[...] = parts[0][...]
        return
    for parity, part in enumerate(parts):
        fill_parity(target, part, chan_count, parity)


def fill_parity(target, part, chan_count, parity):
    own = lax.rem(lax.axis_index("chan"), 2)
    first = own if parity == 0 else 1 - own
    rows = target.shape[2] // chan_count
    for source in range(chan_count // 2):
        span = pl.ds(pl.multiple_of((2 * source + first) * rows, rows), rows)
        target[:, :, span, :] = part[:, :, pl.ds(source * rows, rows), :]


def round_of(pairing_ref, mask):
    rounds = lax.broadcasted_iota(jnp.int32, pairing_ref.shape, 1)
    return jnp.max(jnp.where(pairing_ref[...] == mask, rounds, 0))


def first_kernel(chan_count, block_bits, count, mask, pairing_ref, *refs):
    inputs = [refs[at * count : (at + 1) * count] for at in range(3)]
    block, autos_hbm, vis_hbm, partner, autos, vis, sems, vis_sems = refs[3 * count :]
    half = block.shape[1]
    top = bit_of(lax.axis_index("inp"), block_bits - 1)
    copies = []

    def store(source, target, sem):
        copy = pltpu.make_async_copy(source, target, sem)
        copy.start()
        copies.append(copy)

    for slot in range(2):
        fill(block.at[slot], inputs[slot], chan_count)
        for group in range(half):
            rows = block[slot, group]
            autos[0, slot, group], autos[1, slot, group] = products(rows, rows)
        place = pl.ds(half * (slot * top + (1 - slot) * (1 - top)), half)
        for part in range(2):
            store(autos.at[part, slot], autos_hbm.at[part, place], sems.at[part, slot])
    fill(partner, inputs[2], chan_count)
    for group in range(half):
        vis[0, group], vis[1, group] = products(block[1, group], partner[group])
    place = round_of(pairing_ref, mask)
    for part in range(2):
        store(vis.at[part], vis_hbm.at[part, place], vis_sems.at[part])
    for copy in copies:
        copy.wait()


def first_call(pairing, operands, mask, chan_count, block_bits):
    half, slices, rows = operands[0].shape[:3]
    count = len(operands) // 3
    rows *= count
    auto_shape = (2, 2, half, rows, rows)
    block_shape = (2, half, slices, rows, LANES)
    return pl.pallas_call(
        functools.partial(first_kernel, chan_count, block_bits, count, mask),
        out_shape=[
            jax.ShapeDtypeStruct(block_shape, jnp.bfloat16),
            jax.ShapeDtypeStruct((2, 2 * half, rows, rows), jnp.float32),
            jax.ShapeDtypeStruct((2, pairing.shape[1], half, rows, rows), jnp.float32),
        ],
        in_specs=[pl.BlockSpec(memory_space=pltpu.VMEM)] * (1 + len(operands)),
        out_specs=[pl.BlockSpec(memory_space=pltpu.VMEM)]
        + [pl.BlockSpec(memory_space=pltpu.HBM)] * 2,
        scratch_shapes=[
            pltpu.VMEM(block_shape[1:], jnp.bfloat16),
            pltpu.VMEM(auto_shape, jnp.float32),
            pltpu.VMEM((2, half, rows, rows), jnp.float32),
            pltpu.SemaphoreType.DMA((2, 2)),
            pltpu.SemaphoreType.DMA((2,)),
        ],
        compiler_params=pltpu.CompilerParams(vmem_limit_bytes=12 * MIB),
        cost_estimate=pl.CostEstimate(flops=1 << 20, bytes_accessed=4 << 20, transcendentals=0),
        name="correlate_first",
    )(pairing, *operands)


def parts_of(layout, refs):
    found, at = [], 0
    for kind in layout:
        if kind == "stack":
            found.append([refs[at].at[0], refs[at].at[1]])
            at += 1
        else:
            count = 2 if kind == "pair" else 1
            found.append(list(refs[at : at + count]))
            at += count
    return found


def fill_parity_kernel(chan_count, parity, *refs):
    for index, part in enumerate(refs[: -1 - parity]):
        fill_parity(refs[-1].at[index], part, chan_count, parity)


def fill_kernel(*refs):
    for index, part in enumerate(refs[:-1]):
        refs[-1][index] = part[...]


def cross_kernel(chan_count, block_bits, early, late, layout, pairing_ref, block, filled, *refs):
    inputs, refs = refs[: -len(SCRATCH) - 1], refs[-len(SCRATCH) :]
    vis_hbm, others, vis, vis_sems = refs
    own = lax.axis_index("inp")
    top = bit_of(own, block_bits - 1)
    half = block.shape[1]
    for index, parts in enumerate(parts_of(layout, inputs)):
        fill(others.at[index], parts, chan_count)
    partners = [(mask, filled.at[at]) for at, mask in enumerate(early)]
    partners += [(mask, others.at[at]) for at, mask in enumerate(late)]
    copies = []
    for index, (mask, other) in enumerate(partners):
        bit = top_bit(mask)
        slot = 1
        if bit != block_bits - 1:
            slot = (bit_of(own, bit) == top).astype(jnp.int32)
        for group in range(half):
            vis[0, index, group], vis[1, index, group] = products(block[slot, group], other[group])
        place = round_of(pairing_ref, mask)
        for part in range(2):
            copy = pltpu.make_async_copy(
                vis.at[part, index], vis_hbm.at[part, place], vis_sems.at[part, index]
            )
            copy.start()
            copies.append(copy)
    for copy in copies:
        copy.wait()


SCRATCH = ("vis_hbm", "others", "vis", "vis_sems")


def cross_call(pairing, block, visibilities, received, early, late, chan_count, block_bits):
    _, half, slices, rows, _ = block.shape
    filled_shape = (len(early),) + block.shape[1:]
    cost = functools.partial(pl.CostEstimate, transcendentals=0)
    if received[early[0]][0] == "pair":
        filled = []
        for parity in range(2):
            filled = vmem_call(
                "fill_far" if parity else "fill_near",
                functools.partial(fill_parity_kernel, chan_count, parity),
                [filled_shape],
                [received[mask][1][parity] for mask in early] + list(filled),
                cost=cost(flops=FILL_FLOPS[parity], bytes_accessed=1 << 20),
                aliases={len(early): 0} if parity else None,
            )
    else:
        filled = vmem_call(
            "fill", fill_kernel, [filled_shape], [received[mask][1][0] for mask in early]
        )
    (filled,) = filled
    layout = tuple(received[mask][0] for mask in late)
    operands = [value for mask in late for value in received[mask][1]]
    count = len(early) + len(late)
    vis_shape = (2, count, half, rows, rows)
    return pl.pallas_call(
        functools.partial(cross_kernel, chan_count, block_bits, early, late, layout),
        out_shape=jax.ShapeDtypeStruct(visibilities.shape, jnp.float32),
        in_specs=[pl.BlockSpec(memory_space=pltpu.VMEM)] * (3 + len(operands))
        + [pl.BlockSpec(memory_space=pltpu.HBM)],
        out_specs=pl.BlockSpec(memory_space=pltpu.HBM),
        input_output_aliases={3 + len(operands): 0},
        scratch_shapes=[
            pltpu.VMEM((len(late), half, slices, rows, LANES), jnp.bfloat16),
            pltpu.VMEM(vis_shape, jnp.float32),
            pltpu.SemaphoreType.DMA(vis_shape[:2]),
        ],
        compiler_params=pltpu.CompilerParams(vmem_limit_bytes=16 * MIB),
        cost_estimate=pl.CostEstimate(
            flops=16 * count * half * rows * rows * slices * LANES,
            bytes_accessed=4 << 20,
            transcendentals=0,
        ),
        name="cross",
    )(pairing, block, filled, *operands, visibilities)


def on_device(voltages, filter_taps, pairing):
    pairing = pairing[None, :]
    chan_count = lax.axis_size("chan")
    inp_count = lax.axis_size("inp")
    block_bits = top_bit(inp_count)
    own_chan = lax.axis_index("chan")
    signals = voltages.shape[1]

    def exchange(value, axis, mask):
        count = lax.axis_size(axis)
        return lax.ppermute(value, axis, [(i, i ^ mask) for i in range(count)])

    evens = hops(chan_count)[1:]

    def along(values):
        return [exchange(value, "chan", k) for value, k in zip(values, evens)]

    own_moving, own_other, direct, held, relay_moving, relay_other = spectra_pieces(
        voltages, filter_taps, chan_count
    )
    part = own_moving.shape
    half = part[0]
    relay_moving = exchange(relay_moving, "chan", 1)
    direct = along(direct)
    relay_other = exchange(relay_other, "chan", 1)
    far_own, *onward = vmem_call(
        "split", split_kernel, [part] * (chan_count // 2), [relay_moving]
    )
    onward = along(onward)
    near, far = [own_moving] + direct, [far_own] + onward
    laid = part[:2] + (chan_count // 2 * signals, LANES)
    whole_tiles = signals % ROWS == 0
    top_mask = inp_count // 2
    if not whole_tiles:
        ordered = np.argsort(hops(chan_count))
        sources = jnp.bitwise_xor(own_chan // 2, jnp.arange(chan_count // 2))

        def merge(parts):
            parts = [parts[at] for at in ordered]
            return jnp.take(jnp.stack(parts, axis=2), sources, axis=2).reshape(laid)

        near, far = [merge(near)], [merge(far)]
    (near,) = vmem_call("near", lay_kernel, [laid], near)
    crossed = [exchange(near, "inp", top_mask)]
    (far,) = vmem_call("far", lay_kernel, [laid], far)
    crossed.append(exchange(far, "inp", top_mask))
    rest = vmem_call(
        "hand_on",
        hand_on_kernel,
        [(2,) + part] * len(evens),
        [held, relay_other],
        [near],
    )
    rest = along(rest)
    if whole_tiles:
        other_kernel = functools.partial(lay_rest_kernel, len(evens))
        others = [own_other, relay_other] + rest
    else:
        other_kernel = functools.partial(lay_other_kernel, 1)
        others = [
            merge([own_other] + [value[0] for value in rest]),
            merge([relay_other[0]] + [value[1] for value in rest]),
        ]
    near_other, far_other, *sends = vmem_call(
        "other",
        other_kernel,
        [laid] * 2 + [(2,) + laid] * (block_bits - 1),
        [near, far] + others,
    )
    masks = list(range(1, inp_count))
    received = {top_mask: ("pair", crossed)}
    for mask in masks:
        bit = top_bit(mask)
        if mask == top_mask:
            continue
        if mask > 1 and mask % 2:
            kind, values = received[mask - 1]
            received[mask] = (kind, [exchange(value, "inp", 1) for value in values])
        else:
            kind, values = "pair", [near, far]
            if bit != block_bits - 1:
                kind, values = "stack", [sends[bit]]
            received[mask] = (kind, [exchange(value, "inp", mask) for value in values])
    block = [("pair", [near, far]), ("pair", [near_other, far_other])]
    if not whole_tiles:
        parities = jnp.bitwise_xor(own_chan % 2, jnp.arange(2))

        def interleave(entry):
            kind, values = entry
            if kind == "stack":
                values = [values[0][0], values[0][1]]
            shaped = [value.reshape(half, -1, chan_count // 2, signals, LANES) for value in values]
            ordered = jnp.take(jnp.stack(shaped, axis=3), parities, axis=3)
            return ("whole", [ordered.reshape(half, -1, chan_count * signals, LANES)])

        block = [interleave(entry) for entry in block]
        received = {mask: interleave(entry) for mask, entry in received.items()}
    early = [mask for mask in masks if mask > top_mask]
    late = [mask for mask in masks if mask < top_mask]
    rows, autos, visibilities = first_call(
        pairing,
        [value for _, values in block + [received[top_mask]] for value in values],
        top_mask,
        chan_count,
        block_bits,
    )
    visibilities = cross_call(
        pairing, rows, visibilities, received, early, late, chan_count, block_bits
    )
    return (visibilities, autos)


def solution(mesh):
    in_specs = (P(None, ("inp", "chan"), None), P(), P())
    out_specs = (P(None, None, "chan", "inp", None), P(None, "chan", "inp", None))
    return jax.shard_map(
        on_device, mesh=mesh, in_specs=in_specs, out_specs=out_specs, check_vma=False
    )
```

```python
import functools
import math

import jax
import jax.numpy as jnp
import numpy as np
from jax import lax
from jax.experimental import pallas as pl
from jax.experimental.pallas import tpu as pltpu
from jax.sharding import PartitionSpec as P

AVG = 64
LANES = 128
OUTER = 32
ROWS = 16
MIB = 1024 * 1024
FILL_FLOPS = (9 << 26, 9 << 27)


def twiddle_table():
    fine = OUTER * LANES
    k1 = np.arange(OUTER)[None, :, None]
    odd = np.arange(2)[:, None, None]
    q = np.arange(LANES)[None, None, :]
    turned = k1 + OUTER * ((-4 * k1 - 2 * odd) % LANES)
    angle = (turned * q % fine) * (2.0 * math.pi / fine)
    return np.concatenate([np.cos(angle), np.sin(angle)], axis=2).astype(np.float32)


def lane_matrix():
    fine = OUTER * LANES
    q = np.arange(LANES)
    angle = (q[:, None] * q[None, :] % LANES) * (2.0 * math.pi / LANES)
    cos, sin = np.cos(angle), np.sin(angle)
    return (np.block([[cos, -sin], [sin, cos]]) * fine**-0.5).astype(np.float32)


def add(x, y):
    return (x[0] + y[0], x[1] + y[1])


def sub(x, y):
    return (x[0] - y[0], x[1] - y[1])


def minus_i(x):
    return (x[1], -x[0])


def turn(x, step, count):
    step %= count
    if step == 0:
        return x
    if 4 * step == count:
        return minus_i(x)
    if 8 * step == count:
        half = math.sqrt(0.5)
        return ((x[0] + x[1]) * half, (x[1] - x[0]) * half)
    if 8 * step == 3 * count:
        half = math.sqrt(0.5)
        return ((x[1] - x[0]) * half, (x[0] + x[1]) * -half)
    cos, sin = math.cos(2 * math.pi * step / count), math.sin(2 * math.pi * step / count)
    return (x[0] * cos + x[1] * sin, x[1] * cos - x[0] * sin)


def four(x):
    even, odd = add(x[0], x[2]), sub(x[0], x[2])
    other, last = add(x[1], x[3]), minus_i(sub(x[1], x[3]))
    return [add(even, other), add(odd, last), sub(even, other), sub(odd, last)]


def eight(x):
    even, odd = four(x[0::2]), four(x[1::2])
    odd = [turn(value, k, 8) for k, value in enumerate(odd)]
    return [add(e, o) for e, o in zip(even, odd)] + [sub(e, o) for e, o in zip(even, odd)]


def bit_of(value, bit):
    return lax.rem(lax.div(value, 1 << bit), 2)


def top_bit(count):
    return count.bit_length() - 1


def hops(count):
    return [0] + sorted(range(2, count, 2), key=lambda hop: (-top_bit(hop), hop))


def frame_loads(frame_count):
    bounds = [0] + list(range(5, frame_count, 7)) + [frame_count]
    return list(zip(bounds[:-1], bounds[1:]))


def spectra_kernel(chan_count, spectra_count, volt_hbm, taps_hbm, table_hbm, *refs):
    outs, scratch = refs[:-10], refs[-10:]
    volt_ref, taps_ref, table_ref, matrix_ref = scratch[:4]
    filtered, first, last, pieces, volt_sems, table_sems = scratch[4:]
    tap_count, fine = taps_ref.shape
    frame_count = spectra_count + tap_count - 1
    loads = frame_loads(frame_count)
    volt_copies = []
    for at, (begin, end) in enumerate(loads):
        span = pl.ds(begin * fine, (end - begin) * fine)
        volt_copies.append(
            pltpu.make_async_copy(
                volt_hbm.at[:, :, span], volt_ref.at[:, :, span], volt_sems.at[at]
            )
        )
    table_copies = [
        pltpu.make_async_copy(source, target, table_sems.at[at])
        for at, (source, target) in enumerate(
            [(taps_hbm, taps_ref), (table_hbm, table_ref)]
        )
    ]
    volt_copies[0].start()
    table_copies[0].start()
    for copy in volt_copies[1:]:
        copy.start()
    table_copies[1].start()
    for at, (begin, end) in enumerate(loads):
        if at == 0:
            table_copies[0].wait()
        volt_copies[at].wait()

        def filter_column(p, carry, begin=begin, end=end):
            column = pl.multiple_of(p * LANES, LANES)
            taps = {}
            for t in range(max(0, begin - spectra_count + 1), min(tap_count, end)):
                taps[t] = taps_ref[pl.ds(t, 1), pl.ds(column, LANES)]
            for part in range(2):
                sums = {}
                for frame in range(begin, end):
                    lane = pl.multiple_of(frame * fine + column, LANES)
                    values = volt_ref[part, :, pl.ds(lane, LANES)].astype(jnp.float32)
                    for s in range(spectra_count):
                        if 0 <= frame - s < tap_count:
                            term = taps[frame - s] * values
                            if s not in sums and frame > s:
                                sums[s] = filtered[s, part, p]
                            sums[s] = sums[s] + term if s in sums else term
                for s, total in sums.items():
                    filtered[s, part, p] = total
            return carry

        lax.fori_loop(0, OUTER, filter_column, 0, unroll=8)
    table_copies[1].wait()
    table = table_ref[pl.ds(0, 2 * LANES), :]
    matrix_ref[0] = table.astype(jnp.bfloat16)
    matrix_ref[1] = (table - matrix_ref[0].astype(jnp.float32)).astype(jnp.bfloat16)

    def transform(s, carry):
        for a in range(8):
            values = four([(filtered[s, 0, a + 8 * b], filtered[s, 1, a + 8 * b]) for b in range(4)])
            for r in range(4):
                real, imag = turn(values[r], a * r, OUTER)
                first[0, r, a] = real
                first[1, r, a] = imag
        odd = s % 2
        for r in range(4):
            values = eight([(first[0, r, a], first[1, r, a]) for a in range(8)])
            highs, lows = [], []
            for t in range(8):
                k1 = r + 4 * t
                factors = table_ref[pl.ds(2 * LANES + odd * OUTER + k1, 1), :]
                cos, sin = factors[:, :LANES], factors[:, LANES:]
                real, imag = values[t]
                row = jnp.concatenate([real * cos + imag * sin, imag * cos - real * sin], axis=1)
                high = row.astype(jnp.bfloat16)
                highs.append(high)
                lows.append((row - high.astype(jnp.float32)).astype(jnp.bfloat16))
            high = jnp.concatenate(highs, axis=0)
            low = jnp.concatenate(lows, axis=0)
            dot = functools.partial(jnp.dot, preferred_element_type=jnp.float32)
            result = dot(high, matrix_ref[0]) + (dot(low, matrix_ref[0]) + dot(high, matrix_ref[1]))
            result = result.astype(jnp.bfloat16)
            for t in range(8):
                rows = result[t * ROWS : (t + 1) * ROWS]
                last[s, 0, r + 4 * t] = rows[:, :LANES]
                last[s, 1, r + 4 * t] = rows[:, LANES:]
        return carry


    lane = lax.broadcasted_iota(jnp.int32, (ROWS, LANES), 1)
    bits = [(lane >> bit) & 1 == 1 for bit in range(7)]
    group_count = pieces.shape[1]

    def regroup(part, pair):
        even = [last[2 * pair, part, k1] for k1 in range(OUTER)]
        odd = [last[2 * pair + 1, part, k1] for k1 in range(OUTER)]
        mixed = [
            [jnp.where(bits[1], odd[v], even[v]) for v in range(OUTER)],
            [jnp.where(bits[1], even[v], odd[v - 1]) for v in range(OUTER)],
        ]
        for which in range(2):
            tiles = [mixed[which][-v % OUTER] for v in range(OUTER)]
            for bit in range(5):
                tiles = [
                    jnp.where(bits[2 + bit], tiles[v - (1 << bit)], tiles[v])
                    for v in range(OUTER)
                ]
            for u in range(OUTER):
                chan, group = divmod(2 * u + which, group_count)
                pieces[chan, group, part * (spectra_count // 2) + pair] = tiles[u]

    for s in range(spectra_count):
        transform(s, 0)
        if s % 2:
            regroup(0, s // 2)
            regroup(1, s // 2)

    own = lax.axis_index("chan")
    top = bit_of(lax.axis_index("inp"), top_bit(lax.axis_size("inp")) - 1)
    half = group_count // 2
    moving, other = pl.ds((1 - top) * half, half), pl.ds(top * half, half)
    own_moving, own_other, *direct, held, relay_moving, relay_other = outs
    own_moving[...] = pieces[own, moving]
    own_other[...] = pieces[own, other]
    for index, hop in enumerate(hops(chan_count)):
        chan = jnp.bitwise_xor(own, hop)
        if index:
            direct[index - 1][...] = pieces[chan, moving]
            held[index - 1] = pieces[chan, other]
        relay_moving[index] = pieces[jnp.bitwise_xor(chan, 1), moving]
        relay_other[index] = pieces[jnp.bitwise_xor(chan, 1), other]


def spectra_pieces(voltages, filter_taps, chan_count):
    tap_count, fine = filter_taps.shape
    signals = voltages.shape[1]
    spectra_count = voltages.shape[2] // fine - tap_count + 1
    padded = -signals % ROWS
    if padded:
        voltages = jnp.pad(voltages, ((0, 0), (0, padded), (0, 0)))
    group_count = fine // AVG // chan_count
    slices = spectra_count
    piece = (group_count, slices, ROWS, LANES)
    part = (group_count // 2, slices, ROWS, LANES)
    half_count = chan_count // 2
    shapes = [part] * (half_count + 1) + [(half_count - 1,) + part] + [(half_count,) + part] * 2
    table = np.concatenate([lane_matrix(), twiddle_table().reshape(-1, 2 * LANES)])
    outs = pl.pallas_call(
        functools.partial(spectra_kernel, chan_count, spectra_count),
        out_shape=[jax.ShapeDtypeStruct(shape, jnp.bfloat16) for shape in shapes],
        in_specs=[pl.BlockSpec(memory_space=pltpu.HBM)] * 3,
        out_specs=[pl.BlockSpec(memory_space=pltpu.VMEM)] * len(shapes),
        scratch_shapes=[
            pltpu.VMEM(voltages.shape, jnp.bfloat16),
            pltpu.VMEM(filter_taps.shape, jnp.float32),
            pltpu.VMEM(table.shape, jnp.float32),
            pltpu.VMEM((2, 2 * LANES, 2 * LANES), jnp.bfloat16),
            pltpu.VMEM((spectra_count, 2, OUTER, ROWS, LANES), jnp.float32),
            pltpu.VMEM((2, 4, 8, ROWS, LANES), jnp.float32),
            pltpu.VMEM((spectra_count, 2, OUTER, ROWS, LANES), jnp.bfloat16),
            pltpu.VMEM((chan_count,) + piece, jnp.bfloat16),
            pltpu.SemaphoreType.DMA((len(frame_loads(spectra_count + tap_count - 1)),)),
            pltpu.SemaphoreType.DMA((2,)),
        ],
        compiler_params=pltpu.CompilerParams(vmem_limit_bytes=53 * MIB),
        name="spectra",
    )(voltages, filter_taps, jnp.asarray(table))
    outs = [out[..., :signals, :] for out in outs]
    return outs[:2] + [outs[2:-3]] + outs[-3:]


def vmem_call(name, kernel, out_shapes, operands, after=(), cost=None, aliases=None):
    count = len(operands)
    operands = list(operands) + list(after)

    def body(*refs):
        kernel(*refs[:count], *refs[len(operands) :])

    return pl.pallas_call(
        body,
        out_shape=[jax.ShapeDtypeStruct(shape, jnp.bfloat16) for shape in out_shapes],
        in_specs=[pl.BlockSpec(memory_space=pltpu.VMEM)] * count
        + [pl.BlockSpec(memory_space=pl.ANY)] * len(after),
        out_specs=[pl.BlockSpec(memory_space=pltpu.VMEM)] * len(out_shapes),
        compiler_params=pltpu.CompilerParams(vmem_limit_bytes=8 * MIB),
        cost_estimate=cost,
        input_output_aliases=aliases or {},
        name=name,
    )(*operands)


def split_kernel(relayed, *outs):
    for index, out in enumerate(outs):
        out[...] = relayed[index]


def hand_on_kernel(held, relayed, *outs):
    for index, out in enumerate(outs):
        out[0] = held[index]
        out[1] = relayed[index + 1]


def lay(out, pieces):
    count = len(pieces)
    if count == 1:
        out[...] = pieces[0][...]
        return
    own = lax.axis_index("chan")
    rows = out.shape[2] // count
    for hop, piece in zip(hops(2 * count), pieces):
        source = lax.div(jnp.bitwise_xor(own, hop), 2)
        span = pl.ds(pl.multiple_of(source * rows, rows), rows)
        out[:, :, span, :] = piece[...]


def lay_kernel(*refs):
    lay(refs[-1], refs[:-1])


def lay_rest_kernel(rest_count, near_moving, far_moving, own_other, relayed, *refs):
    rest, outs = refs[:rest_count], refs[rest_count:]
    near = [own_other] + [value.at[0] for value in rest]
    far = [relayed.at[0]] + [value.at[1] for value in rest]
    lay_other_kernel(len(near), near_moving, far_moving, *near, *far, *outs)


def lay_other_kernel(piece_count, near_moving, far_moving, *refs):
    near, far = refs[:piece_count], refs[piece_count : 2 * piece_count]
    near_other, far_other, *sends = refs[2 * piece_count :]
    lay(near_other, near)
    lay(far_other, far)
    block = lax.axis_index("inp")
    top = bit_of(block, len(sends))
    for bit, out in enumerate(sends):
        same = bit_of(block, bit) == top

        @pl.when(same)
        def _(out=out):
            out[0] = near_moving[...]
            out[1] = far_moving[...]

        @pl.when(jnp.logical_not(same))
        def _(out=out):
            out[0] = near_other[...]
            out[1] = far_other[...]


def products(left, right):
    slices, rows, _ = left.shape

    def operand(values):
        part = slices // 2
        real = jnp.concatenate([values[i] for i in range(part)], axis=1)
        imag = jnp.concatenate([values[i] for i in range(part, slices)], axis=1)
        return jnp.concatenate([real, imag], axis=0)

    contract = (((1,), (1,)), ((), ()))
    all_parts = lax.dot_general(
        operand(left), operand(right), contract, preferred_element_type=jnp.float32
    )
    scale = 2.0 / (slices * LANES)
    real = all_parts[:rows, :rows] + all_parts[rows:, rows:]
    imag = all_parts[rows:, :rows] - all_parts[:rows, rows:]
    return real * scale, imag * scale


def fill(target, parts, chan_count):
    if len(parts) == 1:
        target[...] = parts[0][...]
        return
    for parity, part in enumerate(parts):
        fill_parity(target, part, chan_count, parity)


def fill_parity(target, part, chan_count, parity):
    own = lax.rem(lax.axis_index("chan"), 2)
    first = own if parity == 0 else 1 - own
    rows = target.shape[2] // chan_count
    for source in range(chan_count // 2):
        span = pl.ds(pl.multiple_of((2 * source + first) * rows, rows), rows)
        target[:, :, span, :] = part[:, :, pl.ds(source * rows, rows), :]


def round_of(pairing_ref, mask):
    rounds = lax.broadcasted_iota(jnp.int32, pairing_ref.shape, 1)
    return jnp.max(jnp.where(pairing_ref[...] == mask, rounds, 0))


def first_kernel(chan_count, block_bits, count, mask, pairing_ref, *refs):
    inputs = [refs[at * count : (at + 1) * count] for at in range(3)]
    block, autos_hbm, vis_hbm, partner, autos, vis, sems, vis_sems = refs[3 * count :]
    half = block.shape[1]
    top = bit_of(lax.axis_index("inp"), block_bits - 1)
    copies = []

    def store(source, target, sem):
        copy = pltpu.make_async_copy(source, target, sem)
        copy.start()
        copies.append(copy)

    for slot in range(2):
        fill(block.at[slot], inputs[slot], chan_count)
        for group in range(half):
            rows = block[slot, group]
            autos[0, slot, group], autos[1, slot, group] = products(rows, rows)
        place = pl.ds(half * (slot * top + (1 - slot) * (1 - top)), half)
        for part in range(2):
            store(autos.at[part, slot], autos_hbm.at[part, place], sems.at[part, slot])
    fill(partner, inputs[2], chan_count)
    for group in range(half):
        vis[0, group], vis[1, group] = products(block[1, group], partner[group])
    place = round_of(pairing_ref, mask)
    for part in range(2):
        store(vis.at[part], vis_hbm.at[part, place], vis_sems.at[part])
    for copy in copies:
        copy.wait()


def first_call(pairing, operands, mask, chan_count, block_bits):
    half, slices, rows = operands[0].shape[:3]
    count = len(operands) // 3
    rows *= count
    auto_shape = (2, 2, half, rows, rows)
    block_shape = (2, half, slices, rows, LANES)
    return pl.pallas_call(
        functools.partial(first_kernel, chan_count, block_bits, count, mask),
        out_shape=[
            jax.ShapeDtypeStruct(block_shape, jnp.bfloat16),
            jax.ShapeDtypeStruct((2, 2 * half, rows, rows), jnp.float32),
            jax.ShapeDtypeStruct((2, pairing.shape[1], half, rows, rows), jnp.float32),
        ],
        in_specs=[pl.BlockSpec(memory_space=pltpu.VMEM)] * (1 + len(operands)),
        out_specs=[pl.BlockSpec(memory_space=pltpu.VMEM)]
        + [pl.BlockSpec(memory_space=pltpu.HBM)] * 2,
        scratch_shapes=[
            pltpu.VMEM(block_shape[1:], jnp.bfloat16),
            pltpu.VMEM(auto_shape, jnp.float32),
            pltpu.VMEM((2, half, rows, rows), jnp.float32),
            pltpu.SemaphoreType.DMA((2, 2)),
            pltpu.SemaphoreType.DMA((2,)),
        ],
        compiler_params=pltpu.CompilerParams(vmem_limit_bytes=12 * MIB),
        cost_estimate=pl.CostEstimate(flops=1 << 20, bytes_accessed=4 << 20, transcendentals=0),
        name="correlate_first",
    )(pairing, *operands)


def parts_of(layout, refs):
    found, at = [], 0
    for kind in layout:
        if kind == "stack":
            found.append([refs[at].at[0], refs[at].at[1]])
            at += 1
        else:
            count = 2 if kind == "pair" else 1
            found.append(list(refs[at : at + count]))
            at += count
    return found


def fill_parity_kernel(chan_count, parity, *refs):
    for index, part in enumerate(refs[: -1 - parity]):
        fill_parity(refs[-1].at[index], part, chan_count, parity)


def fill_kernel(*refs):
    for index, part in enumerate(refs[:-1]):
        refs[-1][index] = part[...]


def cross_kernel(chan_count, block_bits, early, late, layout, pairing_ref, block, filled, *refs):
    inputs, refs = refs[: -len(SCRATCH) - 1], refs[-len(SCRATCH) :]
    vis_hbm, others, vis, vis_sems = refs
    own = lax.axis_index("inp")
    top = bit_of(own, block_bits - 1)
    half = block.shape[1]
    for index, parts in enumerate(parts_of(layout, inputs)):
        fill(others.at[index], parts, chan_count)
    partners = [(mask, filled.at[at]) for at, mask in enumerate(early)]
    partners += [(mask, others.at[at]) for at, mask in enumerate(late)]
    copies = []
    for index, (mask, other) in enumerate(partners):
        bit = top_bit(mask)
        slot = 1
        if bit != block_bits - 1:
            slot = (bit_of(own, bit) == top).astype(jnp.int32)
        place = round_of(pairing_ref, mask)
        for group in range(half):
            vis[0, index, group], vis[1, index, group] = products(block[slot, group], other[group])
            copy = pltpu.make_async_copy(
                vis.at[:, index, group], vis_hbm.at[:, place, group], vis_sems.at[index, group]
            )
            copy.start()
            copies.append(copy)
    for copy in copies:
        copy.wait()


SCRATCH = ("vis_hbm", "others", "vis", "vis_sems")


def cross_call(pairing, block, visibilities, received, early, late, chan_count, block_bits):
    _, half, slices, rows, _ = block.shape
    filled_shape = (len(early),) + block.shape[1:]
    cost = functools.partial(pl.CostEstimate, transcendentals=0)
    if received[early[0]][0] == "pair":
        filled = []
        for parity in range(2):
            filled = vmem_call(
                "fill_far" if parity else "fill_near",
                functools.partial(fill_parity_kernel, chan_count, parity),
                [filled_shape],
                [received[mask][1][parity] for mask in early] + list(filled),
                cost=cost(flops=FILL_FLOPS[parity], bytes_accessed=1 << 20),
                aliases={len(early): 0} if parity else None,
            )
    else:
        filled = vmem_call(
            "fill", fill_kernel, [filled_shape], [received[mask][1][0] for mask in early]
        )
    (filled,) = filled
    layout = tuple(received[mask][0] for mask in late)
    operands = [value for mask in late for value in received[mask][1]]
    count = len(early) + len(late)
    vis_shape = (2, count, half, rows, rows)
    return pl.pallas_call(
        functools.partial(cross_kernel, chan_count, block_bits, early, late, layout),
        out_shape=jax.ShapeDtypeStruct(visibilities.shape, jnp.float32),
        in_specs=[pl.BlockSpec(memory_space=pltpu.VMEM)] * (3 + len(operands))
        + [pl.BlockSpec(memory_space=pltpu.HBM)],
        out_specs=pl.BlockSpec(memory_space=pltpu.HBM),
        input_output_aliases={3 + len(operands): 0},
        scratch_shapes=[
            pltpu.VMEM((len(late), half, slices, rows, LANES), jnp.bfloat16),
            pltpu.VMEM(vis_shape, jnp.float32),
            pltpu.SemaphoreType.DMA(vis_shape[1:3]),
        ],
        compiler_params=pltpu.CompilerParams(vmem_limit_bytes=16 * MIB),
        cost_estimate=pl.CostEstimate(
            flops=16 * count * half * rows * rows * slices * LANES,
            bytes_accessed=4 << 20,
            transcendentals=0,
        ),
        name="cross",
    )(pairing, block, filled, *operands, visibilities)


def on_device(voltages, filter_taps, pairing):
    pairing = pairing[None, :]
    chan_count = lax.axis_size("chan")
    inp_count = lax.axis_size("inp")
    block_bits = top_bit(inp_count)
    own_chan = lax.axis_index("chan")
    signals = voltages.shape[1]

    def exchange(value, axis, mask):
        count = lax.axis_size(axis)
        return lax.ppermute(value, axis, [(i, i ^ mask) for i in range(count)])

    evens = hops(chan_count)[1:]

    def along(values):
        return [exchange(value, "chan", k) for value, k in zip(values, evens)]

    own_moving, own_other, direct, held, relay_moving, relay_other = spectra_pieces(
        voltages, filter_taps, chan_count
    )
    part = own_moving.shape
    half = part[0]
    relay_moving = exchange(relay_moving, "chan", 1)
    direct = along(direct)
    relay_other = exchange(relay_other, "chan", 1)
    far_own, *onward = vmem_call(
        "split", split_kernel, [part] * (chan_count // 2), [relay_moving]
    )
    onward = along(onward)
    near, far = [own_moving] + direct, [far_own] + onward
    laid = part[:2] + (chan_count // 2 * signals, LANES)
    whole_tiles = signals % ROWS == 0
    top_mask = inp_count // 2
    if not whole_tiles:
        ordered = np.argsort(hops(chan_count))
        sources = jnp.bitwise_xor(own_chan // 2, jnp.arange(chan_count // 2))

        def merge(parts):
            parts = [parts[at] for at in ordered]
            return jnp.take(jnp.stack(parts, axis=2), sources, axis=2).reshape(laid)

        near, far = [merge(near)], [merge(far)]
    (near,) = vmem_call("near", lay_kernel, [laid], near)
    crossed = [exchange(near, "inp", top_mask)]
    (far,) = vmem_call("far", lay_kernel, [laid], far)
    crossed.append(exchange(far, "inp", top_mask))
    rest = vmem_call(
        "hand_on",
        hand_on_kernel,
        [(2,) + part] * len(evens),
        [held, relay_other],
        [direct[0]],
    )
    rest = along(rest)
    if whole_tiles:
        other_kernel = functools.partial(lay_rest_kernel, len(evens))
        others = [own_other, relay_other] + rest
    else:
        other_kernel = functools.partial(lay_other_kernel, 1)
        others = [
            merge([own_other] + [value[0] for value in rest]),
            merge([relay_other[0]] + [value[1] for value in rest]),
        ]
    near_other, far_other, *sends = vmem_call(
        "other",
        other_kernel,
        [laid] * 2 + [(2,) + laid] * (block_bits - 1),
        [near, far] + others,
    )
    masks = list(range(1, inp_count))
    received = {top_mask: ("pair", crossed)}
    for mask in masks:
        bit = top_bit(mask)
        if mask == top_mask:
            continue
        if mask > 1 and mask % 2:
            kind, values = received[mask - 1]
            received[mask] = (kind, [exchange(value, "inp", 1) for value in values])
        else:
            kind, values = "pair", [near, far]
            if bit != block_bits - 1:
                kind, values = "stack", [sends[bit]]
            received[mask] = (kind, [exchange(value, "inp", mask) for value in values])
    block = [("pair", [near, far]), ("pair", [near_other, far_other])]
    if not whole_tiles:
        parities = jnp.bitwise_xor(own_chan % 2, jnp.arange(2))

        def interleave(entry):
            kind, values = entry
            if kind == "stack":
                values = [values[0][0], values[0][1]]
            shaped = [value.reshape(half, -1, chan_count // 2, signals, LANES) for value in values]
            ordered = jnp.take(jnp.stack(shaped, axis=3), parities, axis=3)
            return ("whole", [ordered.reshape(half, -1, chan_count * signals, LANES)])

        block = [interleave(entry) for entry in block]
        received = {mask: interleave(entry) for mask, entry in received.items()}
    early = [mask for mask in masks if mask > top_mask]
    late = [mask for mask in masks if mask < top_mask]
    rows, autos, visibilities = first_call(
        pairing,
        [value for _, values in block + [received[top_mask]] for value in values],
        top_mask,
        chan_count,
        block_bits,
    )
    visibilities = cross_call(
        pairing, rows, visibilities, received, early, late, chan_count, block_bits
    )
    return (visibilities, autos)


def solution(mesh):
    in_specs = (P(None, ("inp", "chan"), None), P(), P())
    out_specs = (P(None, None, "chan", "inp", None), P(None, "chan", "inp", None))
    return jax.shard_map(
        on_device, mesh=mesh, in_specs=in_specs, out_specs=out_specs, check_vma=False
    )
```

```python
import functools
import math

import jax
import jax.numpy as jnp
import numpy as np
from jax import lax
from jax.experimental import pallas as pl
from jax.experimental.pallas import tpu as pltpu
from jax.sharding import PartitionSpec as P

AVG = 64
LANES = 128
OUTER = 32
ROWS = 16
MIB = 1024 * 1024
FILL_FLOPS = (9 << 26, 9 << 27)


def twiddle_table():
    fine = OUTER * LANES
    k1 = np.arange(OUTER)[None, :, None]
    odd = np.arange(2)[:, None, None]
    q = np.arange(LANES)[None, None, :]
    turned = k1 + OUTER * ((-4 * k1 - 2 * odd) % LANES)
    angle = (turned * q % fine) * (2.0 * math.pi / fine)
    return np.concatenate([np.cos(angle), np.sin(angle)], axis=2).astype(np.float32)


def lane_matrix():
    fine = OUTER * LANES
    q = np.arange(LANES)
    angle = (q[:, None] * q[None, :] % LANES) * (2.0 * math.pi / LANES)
    cos, sin = np.cos(angle), np.sin(angle)
    return (np.block([[cos, -sin], [sin, cos]]) * fine**-0.5).astype(np.float32)


def add(x, y):
    return (x[0] + y[0], x[1] + y[1])


def sub(x, y):
    return (x[0] - y[0], x[1] - y[1])


def minus_i(x):
    return (x[1], -x[0])


def turn(x, step, count):
    step %= count
    if step == 0:
        return x
    if 4 * step == count:
        return minus_i(x)
    if 8 * step == count:
        half = math.sqrt(0.5)
        return ((x[0] + x[1]) * half, (x[1] - x[0]) * half)
    if 8 * step == 3 * count:
        half = math.sqrt(0.5)
        return ((x[1] - x[0]) * half, (x[0] + x[1]) * -half)
    cos, sin = math.cos(2 * math.pi * step / count), math.sin(2 * math.pi * step / count)
    return (x[0] * cos + x[1] * sin, x[1] * cos - x[0] * sin)


def four(x):
    even, odd = add(x[0], x[2]), sub(x[0], x[2])
    other, last = add(x[1], x[3]), minus_i(sub(x[1], x[3]))
    return [add(even, other), add(odd, last), sub(even, other), sub(odd, last)]


def eight(x):
    even, odd = four(x[0::2]), four(x[1::2])
    odd = [turn(value, k, 8) for k, value in enumerate(odd)]
    return [add(e, o) for e, o in zip(even, odd)] + [sub(e, o) for e, o in zip(even, odd)]


def bit_of(value, bit):
    return lax.rem(lax.div(value, 1 << bit), 2)


def top_bit(count):
    return count.bit_length() - 1


def hops(count):
    return [0] + sorted(range(2, count, 2), key=lambda hop: (-top_bit(hop), hop))


def frame_loads(frame_count):
    bounds = [0] + list(range(5, frame_count, 7)) + [frame_count]
    return list(zip(bounds[:-1], bounds[1:]))


def spectra_kernel(chan_count, spectra_count, volt_hbm, taps_hbm, table_hbm, *refs):
    outs, scratch = refs[:-10], refs[-10:]
    volt_ref, taps_ref, table_ref, matrix_ref = scratch[:4]
    filtered, first, last, pieces, volt_sems, table_sems = scratch[4:]
    tap_count, fine = taps_ref.shape
    frame_count = spectra_count + tap_count - 1
    loads = frame_loads(frame_count)
    volt_copies = []
    for at, (begin, end) in enumerate(loads):
        span = pl.ds(begin * fine, (end - begin) * fine)
        volt_copies.append(
            pltpu.make_async_copy(
                volt_hbm.at[:, :, span], volt_ref.at[:, :, span], volt_sems.at[at]
            )
        )
    table_copies = [
        pltpu.make_async_copy(source, target, table_sems.at[at])
        for at, (source, target) in enumerate(
            [(taps_hbm, taps_ref), (table_hbm, table_ref)]
        )
    ]
    table_copies[0].start()
    volt_copies[0].start()
    for copy in volt_copies[1:]:
        copy.start()
    table_copies[1].start()
    for at, (begin, end) in enumerate(loads):
        if at == 0:
            table_copies[0].wait()
        volt_copies[at].wait()

        def filter_column(p, carry, begin=begin, end=end):
            column = pl.multiple_of(p * LANES, LANES)
            taps = {}
            for t in range(max(0, begin - spectra_count + 1), min(tap_count, end)):
                taps[t] = taps_ref[pl.ds(t, 1), pl.ds(column, LANES)]
            for part in range(2):
                sums = {}
                for frame in range(begin, end):
                    lane = pl.multiple_of(frame * fine + column, LANES)
                    values = volt_ref[part, :, pl.ds(lane, LANES)].astype(jnp.float32)
                    for s in range(spectra_count):
                        if 0 <= frame - s < tap_count:
                            term = taps[frame - s] * values
                            if s not in sums and frame > s:
                                sums[s] = filtered[s, part, p]
                            sums[s] = sums[s] + term if s in sums else term
                for s, total in sums.items():
                    filtered[s, part, p] = total
            return carry

        lax.fori_loop(0, OUTER, filter_column, 0, unroll=8)
    table_copies[1].wait()
    table = table_ref[pl.ds(0, 2 * LANES), :]
    matrix_ref[0] = table.astype(jnp.bfloat16)
    matrix_ref[1] = (table - matrix_ref[0].astype(jnp.float32)).astype(jnp.bfloat16)

    def transform(s, carry):
        for a in range(8):
            values = four([(filtered[s, 0, a + 8 * b], filtered[s, 1, a + 8 * b]) for b in range(4)])
            for r in range(4):
                real, imag = turn(values[r], a * r, OUTER)
                first[0, r, a] = real
                first[1, r, a] = imag
        odd = s % 2
        for r in range(4):
            values = eight([(first[0, r, a], first[1, r, a]) for a in range(8)])
            highs, lows = [], []
            for t in range(8):
                k1 = r + 4 * t
                factors = table_ref[pl.ds(2 * LANES + odd * OUTER + k1, 1), :]
                cos, sin = factors[:, :LANES], factors[:, LANES:]
                real, imag = values[t]
                row = jnp.concatenate([real * cos + imag * sin, imag * cos - real * sin], axis=1)
                high = row.astype(jnp.bfloat16)
                highs.append(high)
                lows.append((row - high.astype(jnp.float32)).astype(jnp.bfloat16))
            high = jnp.concatenate(highs, axis=0)
            low = jnp.concatenate(lows, axis=0)
            dot = functools.partial(jnp.dot, preferred_element_type=jnp.float32)
            result = dot(high, matrix_ref[0]) + (dot(low, matrix_ref[0]) + dot(high, matrix_ref[1]))
            result = result.astype(jnp.bfloat16)
            for t in range(8):
                rows = result[t * ROWS : (t + 1) * ROWS]
                last[s, 0, r + 4 * t] = rows[:, :LANES]
                last[s, 1, r + 4 * t] = rows[:, LANES:]
        return carry


    lane = lax.broadcasted_iota(jnp.int32, (ROWS, LANES), 1)
    bits = [(lane >> bit) & 1 == 1 for bit in range(7)]
    group_count = pieces.shape[1]

    def regroup(part, pair):
        even = [last[2 * pair, part, k1] for k1 in range(OUTER)]
        odd = [last[2 * pair + 1, part, k1] for k1 in range(OUTER)]
        mixed = [
            [jnp.where(bits[1], odd[v], even[v]) for v in range(OUTER)],
            [jnp.where(bits[1], even[v], odd[v - 1]) for v in range(OUTER)],
        ]
        for which in range(2):
            tiles = [mixed[which][-v % OUTER] for v in range(OUTER)]
            for bit in range(5):
                tiles = [
                    jnp.where(bits[2 + bit], tiles[v - (1 << bit)], tiles[v])
                    for v in range(OUTER)
                ]
            for u in range(OUTER):
                chan, group = divmod(2 * u + which, group_count)
                pieces[chan, group, part * (spectra_count // 2) + pair] = tiles[u]

    for s in range(spectra_count):
        transform(s, 0)
        if s % 2:
            regroup(0, s // 2)
            regroup(1, s // 2)

    own = lax.axis_index("chan")
    top = bit_of(lax.axis_index("inp"), top_bit(lax.axis_size("inp")) - 1)
    half = group_count // 2
    moving, other = pl.ds((1 - top) * half, half), pl.ds(top * half, half)
    own_moving, own_other, *direct, held, relay_moving, relay_other = outs
    own_moving[...] = pieces[own, moving]
    own_other[...] = pieces[own, other]
    for index, hop in enumerate(hops(chan_count)):
        chan = jnp.bitwise_xor(own, hop)
        if index:
            direct[index - 1][...] = pieces[chan, moving]
            held[index - 1] = pieces[chan, other]
        relay_moving[index] = pieces[jnp.bitwise_xor(chan, 1), moving]
        relay_other[index] = pieces[jnp.bitwise_xor(chan, 1), other]


def spectra_pieces(voltages, filter_taps, chan_count):
    tap_count, fine = filter_taps.shape
    signals = voltages.shape[1]
    spectra_count = voltages.shape[2] // fine - tap_count + 1
    padded = -signals % ROWS
    if padded:
        voltages = jnp.pad(voltages, ((0, 0), (0, padded), (0, 0)))
    group_count = fine // AVG // chan_count
    slices = spectra_count
    piece = (group_count, slices, ROWS, LANES)
    part = (group_count // 2, slices, ROWS, LANES)
    half_count = chan_count // 2
    shapes = [part] * (half_count + 1) + [(half_count - 1,) + part] + [(half_count,) + part] * 2
    table = np.concatenate([lane_matrix(), twiddle_table().reshape(-1, 2 * LANES)])
    outs = pl.pallas_call(
        functools.partial(spectra_kernel, chan_count, spectra_count),
        out_shape=[jax.ShapeDtypeStruct(shape, jnp.bfloat16) for shape in shapes],
        in_specs=[pl.BlockSpec(memory_space=pltpu.HBM)] * 3,
        out_specs=[pl.BlockSpec(memory_space=pltpu.VMEM)] * len(shapes),
        scratch_shapes=[
            pltpu.VMEM(voltages.shape, jnp.bfloat16),
            pltpu.VMEM(filter_taps.shape, jnp.float32),
            pltpu.VMEM(table.shape, jnp.float32),
            pltpu.VMEM((2, 2 * LANES, 2 * LANES), jnp.bfloat16),
            pltpu.VMEM((spectra_count, 2, OUTER, ROWS, LANES), jnp.float32),
            pltpu.VMEM((2, 4, 8, ROWS, LANES), jnp.float32),
            pltpu.VMEM((spectra_count, 2, OUTER, ROWS, LANES), jnp.bfloat16),
            pltpu.VMEM((chan_count,) + piece, jnp.bfloat16),
            pltpu.SemaphoreType.DMA((len(frame_loads(spectra_count + tap_count - 1)),)),
            pltpu.SemaphoreType.DMA((2,)),
        ],
        compiler_params=pltpu.CompilerParams(vmem_limit_bytes=53 * MIB),
        name="spectra",
    )(voltages, filter_taps, jnp.asarray(table))
    outs = [out[..., :signals, :] for out in outs]
    return outs[:2] + [outs[2:-3]] + outs[-3:]


def vmem_call(name, kernel, out_shapes, operands, after=(), cost=None, aliases=None):
    count = len(operands)
    operands = list(operands) + list(after)

    def body(*refs):
        kernel(*refs[:count], *refs[len(operands) :])

    return pl.pallas_call(
        body,
        out_shape=[jax.ShapeDtypeStruct(shape, jnp.bfloat16) for shape in out_shapes],
        in_specs=[pl.BlockSpec(memory_space=pltpu.VMEM)] * count
        + [pl.BlockSpec(memory_space=pl.ANY)] * len(after),
        out_specs=[pl.BlockSpec(memory_space=pltpu.VMEM)] * len(out_shapes),
        compiler_params=pltpu.CompilerParams(vmem_limit_bytes=8 * MIB),
        cost_estimate=cost,
        input_output_aliases=aliases or {},
        name=name,
    )(*operands)


def split_kernel(relayed, *outs):
    for index, out in enumerate(outs):
        out[...] = relayed[index]


def hand_on_kernel(held, relayed, *outs):
    for index, out in enumerate(outs):
        out[0] = held[index]
        out[1] = relayed[index + 1]


def lay(out, pieces):
    count = len(pieces)
    if count == 1:
        out[...] = pieces[0][...]
        return
    own = lax.axis_index("chan")
    rows = out.shape[2] // count
    for hop, piece in zip(hops(2 * count), pieces):
        source = lax.div(jnp.bitwise_xor(own, hop), 2)
        span = pl.ds(pl.multiple_of(source * rows, rows), rows)
        out[:, :, span, :] = piece[...]


def lay_kernel(*refs):
    lay(refs[-1], refs[:-1])


def lay_rest_kernel(rest_count, near_moving, far_moving, own_other, relayed, *refs):
    rest, outs = refs[:rest_count], refs[rest_count:]
    near = [own_other] + [value.at[0] for value in rest]
    far = [relayed.at[0]] + [value.at[1] for value in rest]
    lay_other_kernel(len(near), near_moving, far_moving, *near, *far, *outs)


def lay_other_kernel(piece_count, near_moving, far_moving, *refs):
    near, far = refs[:piece_count], refs[piece_count : 2 * piece_count]
    near_other, far_other, *sends = refs[2 * piece_count :]
    lay(near_other, near)
    lay(far_other, far)
    block = lax.axis_index("inp")
    top = bit_of(block, len(sends))
    for bit, out in enumerate(sends):
        same = bit_of(block, bit) == top

        @pl.when(same)
        def _(out=out):
            out[0] = near_moving[...]
            out[1] = far_moving[...]

        @pl.when(jnp.logical_not(same))
        def _(out=out):
            out[0] = near_other[...]
            out[1] = far_other[...]


def products(left, right):
    slices, rows, _ = left.shape

    def operand(values):
        part = slices // 2
        real = jnp.concatenate([values[i] for i in range(part)], axis=1)
        imag = jnp.concatenate([values[i] for i in range(part, slices)], axis=1)
        return jnp.concatenate([real, imag], axis=0)

    contract = (((1,), (1,)), ((), ()))
    all_parts = lax.dot_general(
        operand(left), operand(right), contract, preferred_element_type=jnp.float32
    )
    scale = 2.0 / (slices * LANES)
    real = all_parts[:rows, :rows] + all_parts[rows:, rows:]
    imag = all_parts[rows:, :rows] - all_parts[:rows, rows:]
    return real * scale, imag * scale


def fill(target, parts, chan_count):
    if len(parts) == 1:
        target[...] = parts[0][...]
        return
    for parity, part in enumerate(parts):
        fill_parity(target, part, chan_count, parity)


def fill_parity(target, part, chan_count, parity):
    own = lax.rem(lax.axis_index("chan"), 2)
    first = own if parity == 0 else 1 - own
    rows = target.shape[2] // chan_count
    for source in range(chan_count // 2):
        span = pl.ds(pl.multiple_of((2 * source + first) * rows, rows), rows)
        target[:, :, span, :] = part[:, :, pl.ds(source * rows, rows), :]


def round_of(pairing_ref, mask):
    rounds = lax.broadcasted_iota(jnp.int32, pairing_ref.shape, 1)
    return jnp.max(jnp.where(pairing_ref[...] == mask, rounds, 0))


def first_kernel(chan_count, block_bits, count, mask, pairing_ref, *refs):
    inputs = [refs[at * count : (at + 1) * count] for at in range(3)]
    block, autos_hbm, vis_hbm, partner, autos, vis, sems, vis_sems = refs[3 * count :]
    half = block.shape[1]
    top = bit_of(lax.axis_index("inp"), block_bits - 1)
    copies = []

    def store(source, target, sem):
        copy = pltpu.make_async_copy(source, target, sem)
        copy.start()
        copies.append(copy)

    for slot in range(2):
        fill(block.at[slot], inputs[slot], chan_count)
        for group in range(half):
            rows = block[slot, group]
            autos[0, slot, group], autos[1, slot, group] = products(rows, rows)
        place = pl.ds(half * (slot * top + (1 - slot) * (1 - top)), half)
        for part in range(2):
            store(autos.at[part, slot], autos_hbm.at[part, place], sems.at[part, slot])
    fill(partner, inputs[2], chan_count)
    for group in range(half):
        vis[0, group], vis[1, group] = products(block[1, group], partner[group])
    place = round_of(pairing_ref, mask)
    for part in range(2):
        store(vis.at[part], vis_hbm.at[part, place], vis_sems.at[part])
    for copy in copies:
        copy.wait()


def first_call(pairing, operands, mask, chan_count, block_bits):
    half, slices, rows = operands[0].shape[:3]
    count = len(operands) // 3
    rows *= count
    auto_shape = (2, 2, half, rows, rows)
    block_shape = (2, half, slices, rows, LANES)
    return pl.pallas_call(
        functools.partial(first_kernel, chan_count, block_bits, count, mask),
        out_shape=[
            jax.ShapeDtypeStruct(block_shape, jnp.bfloat16),
            jax.ShapeDtypeStruct((2, 2 * half, rows, rows), jnp.float32),
            jax.ShapeDtypeStruct((2, pairing.shape[1], half, rows, rows), jnp.float32),
        ],
        in_specs=[pl.BlockSpec(memory_space=pltpu.VMEM)] * (1 + len(operands)),
        out_specs=[pl.BlockSpec(memory_space=pltpu.VMEM)]
        + [pl.BlockSpec(memory_space=pltpu.HBM)] * 2,
        scratch_shapes=[
            pltpu.VMEM(block_shape[1:], jnp.bfloat16),
            pltpu.VMEM(auto_shape, jnp.float32),
            pltpu.VMEM((2, half, rows, rows), jnp.float32),
            pltpu.SemaphoreType.DMA((2, 2)),
            pltpu.SemaphoreType.DMA((2,)),
        ],
        compiler_params=pltpu.CompilerParams(vmem_limit_bytes=12 * MIB),
        cost_estimate=pl.CostEstimate(flops=1 << 20, bytes_accessed=4 << 20, transcendentals=0),
        name="correlate_first",
    )(pairing, *operands)


def parts_of(layout, refs):
    found, at = [], 0
    for kind in layout:
        if kind == "stack":
            found.append([refs[at].at[0], refs[at].at[1]])
            at += 1
        else:
            count = 2 if kind == "pair" else 1
            found.append(list(refs[at : at + count]))
            at += count
    return found


def fill_parity_kernel(chan_count, parity, *refs):
    for index, part in enumerate(refs[: -1 - parity]):
        fill_parity(refs[-1].at[index], part, chan_count, parity)


def fill_kernel(*refs):
    for index, part in enumerate(refs[:-1]):
        refs[-1][index] = part[...]


def cross_kernel(chan_count, block_bits, early, late, layout, pairing_ref, block, filled, *refs):
    inputs, refs = refs[: -len(SCRATCH) - 1], refs[-len(SCRATCH) :]
    vis_hbm, others, vis, vis_sems = refs
    own = lax.axis_index("inp")
    top = bit_of(own, block_bits - 1)
    half = block.shape[1]
    for index, parts in enumerate(parts_of(layout, inputs)):
        fill(others.at[index], parts, chan_count)
    partners = [(mask, filled.at[at]) for at, mask in enumerate(early)]
    partners += [(mask, others.at[at]) for at, mask in enumerate(late)]
    copies = []
    for index, (mask, other) in enumerate(partners):
        bit = top_bit(mask)
        slot = 1
        if bit != block_bits - 1:
            slot = (bit_of(own, bit) == top).astype(jnp.int32)
        place = round_of(pairing_ref, mask)
        for group in range(half):
            vis[0, index, group], vis[1, index, group] = products(block[slot, group], other[group])
            copy = pltpu.make_async_copy(
                vis.at[:, index, group], vis_hbm.at[:, place, group], vis_sems.at[index, group]
            )
            copy.start()
            copies.append(copy)
    for copy in copies:
        copy.wait()


SCRATCH = ("vis_hbm", "others", "vis", "vis_sems")


def cross_call(pairing, block, visibilities, received, early, late, chan_count, block_bits):
    _, half, slices, rows, _ = block.shape
    filled_shape = (len(early),) + block.shape[1:]
    cost = functools.partial(pl.CostEstimate, transcendentals=0)
    if received[early[0]][0] == "pair":
        filled = []
        for parity in range(2):
            filled = vmem_call(
                "fill_far" if parity else "fill_near",
                functools.partial(fill_parity_kernel, chan_count, parity),
                [filled_shape],
                [received[mask][1][parity] for mask in early] + list(filled),
                cost=cost(flops=FILL_FLOPS[parity], bytes_accessed=1 << 20),
                aliases={len(early): 0} if parity else None,
            )
    else:
        filled = vmem_call(
            "fill", fill_kernel, [filled_shape], [received[mask][1][0] for mask in early]
        )
    (filled,) = filled
    layout = tuple(received[mask][0] for mask in late)
    operands = [value for mask in late for value in received[mask][1]]
    count = len(early) + len(late)
    vis_shape = (2, count, half, rows, rows)
    return pl.pallas_call(
        functools.partial(cross_kernel, chan_count, block_bits, early, late, layout),
        out_shape=jax.ShapeDtypeStruct(visibilities.shape, jnp.float32),
        in_specs=[pl.BlockSpec(memory_space=pltpu.VMEM)] * (3 + len(operands))
        + [pl.BlockSpec(memory_space=pltpu.HBM)],
        out_specs=pl.BlockSpec(memory_space=pltpu.HBM),
        input_output_aliases={3 + len(operands): 0},
        scratch_shapes=[
            pltpu.VMEM((len(late), half, slices, rows, LANES), jnp.bfloat16),
            pltpu.VMEM(vis_shape, jnp.float32),
            pltpu.SemaphoreType.DMA(vis_shape[1:3]),
        ],
        compiler_params=pltpu.CompilerParams(vmem_limit_bytes=16 * MIB),
        cost_estimate=pl.CostEstimate(
            flops=16 * count * half * rows * rows * slices * LANES,
            bytes_accessed=4 << 20,
            transcendentals=0,
        ),
        name="cross",
    )(pairing, block, filled, *operands, visibilities)


def on_device(voltages, filter_taps, pairing):
    pairing = pairing[None, :]
    chan_count = lax.axis_size("chan")
    inp_count = lax.axis_size("inp")
    block_bits = top_bit(inp_count)
    own_chan = lax.axis_index("chan")
    signals = voltages.shape[1]

    def exchange(value, axis, mask):
        count = lax.axis_size(axis)
        return lax.ppermute(value, axis, [(i, i ^ mask) for i in range(count)])

    evens = hops(chan_count)[1:]

    def along(values):
        return [exchange(value, "chan", k) for value, k in zip(values, evens)]

    own_moving, own_other, direct, held, relay_moving, relay_other = spectra_pieces(
        voltages, filter_taps, chan_count
    )
    part = own_moving.shape
    half = part[0]
    relay_moving = exchange(relay_moving, "chan", 1)
    direct = along(direct)
    relay_other = exchange(relay_other, "chan", 1)
    far_own, *onward = vmem_call(
        "split", split_kernel, [part] * (chan_count // 2), [relay_moving]
    )
    onward = along(onward)
    near, far = [own_moving] + direct, [far_own] + onward
    laid = part[:2] + (chan_count // 2 * signals, LANES)
    whole_tiles = signals % ROWS == 0
    top_mask = inp_count // 2
    if not whole_tiles:
        ordered = np.argsort(hops(chan_count))
        sources = jnp.bitwise_xor(own_chan // 2, jnp.arange(chan_count // 2))

        def merge(parts):
            parts = [parts[at] for at in ordered]
            return jnp.take(jnp.stack(parts, axis=2), sources, axis=2).reshape(laid)

        near, far = [merge(near)], [merge(far)]
    (near,) = vmem_call("near", lay_kernel, [laid], near)
    crossed = [exchange(near, "inp", top_mask)]
    (far,) = vmem_call("far", lay_kernel, [laid], far)
    crossed.append(exchange(far, "inp", top_mask))
    rest = vmem_call(
        "hand_on",
        hand_on_kernel,
        [(2,) + part] * len(evens),
        [held, relay_other],
        [direct[0]],
    )
    rest = along(rest)
    if whole_tiles:
        other_kernel = functools.partial(lay_rest_kernel, len(evens))
        others = [own_other, relay_other] + rest
    else:
        other_kernel = functools.partial(lay_other_kernel, 1)
        others = [
            merge([own_other] + [value[0] for value in rest]),
            merge([relay_other[0]] + [value[1] for value in rest]),
        ]
    near_other, far_other, *sends = vmem_call(
        "other",
        other_kernel,
        [laid] * 2 + [(2,) + laid] * (block_bits - 1),
        [near, far] + others,
    )
    masks = list(range(1, inp_count))
    received = {top_mask: ("pair", crossed)}
    for mask in masks:
        bit = top_bit(mask)
        if mask == top_mask:
            continue
        if mask > 1 and mask % 2:
            kind, values = received[mask - 1]
            received[mask] = (kind, [exchange(value, "inp", 1) for value in values])
        else:
            kind, values = "pair", [near, far]
            if bit != block_bits - 1:
                kind, values = "stack", [sends[bit]]
            received[mask] = (kind, [exchange(value, "inp", mask) for value in values])
    block = [("pair", [near, far]), ("pair", [near_other, far_other])]
    if not whole_tiles:
        parities = jnp.bitwise_xor(own_chan % 2, jnp.arange(2))

        def interleave(entry):
            kind, values = entry
            if kind == "stack":
                values = [values[0][0], values[0][1]]
            shaped = [value.reshape(half, -1, chan_count // 2, signals, LANES) for value in values]
            ordered = jnp.take(jnp.stack(shaped, axis=3), parities, axis=3)
            return ("whole", [ordered.reshape(half, -1, chan_count * signals, LANES)])

        block = [interleave(entry) for entry in block]
        received = {mask: interleave(entry) for mask, entry in received.items()}
    early = [mask for mask in masks if mask > top_mask]
    late = [mask for mask in masks if mask < top_mask]
    rows, autos, visibilities = first_call(
        pairing,
        [value for _, values in block + [received[top_mask]] for value in values],
        top_mask,
        chan_count,
        block_bits,
    )
    visibilities = cross_call(
        pairing, rows, visibilities, received, early, late, chan_count, block_bits
    )
    return (visibilities, autos)


def solution(mesh):
    in_specs = (P(None, ("inp", "chan"), None), P(), P())
    out_specs = (P(None, None, "chan", "inp", None), P(None, "chan", "inp", None))
    return jax.shard_map(
        on_device, mesh=mesh, in_specs=in_specs, out_specs=out_specs, check_vma=False
    )
```

```python
import functools
import math

import jax
import jax.numpy as jnp
import numpy as np
from jax import lax
from jax.experimental import pallas as pl
from jax.experimental.pallas import tpu as pltpu
from jax.sharding import PartitionSpec as P

AVG = 64
LANES = 128
OUTER = 32
ROWS = 16
MIB = 1024 * 1024
FILL_FLOPS = (9 << 26, 9 << 27)


def twiddle_table():
    fine = OUTER * LANES
    k1 = np.arange(OUTER)[None, :, None]
    odd = np.arange(2)[:, None, None]
    q = np.arange(LANES)[None, None, :]
    turned = k1 + OUTER * ((-4 * k1 - 2 * odd) % LANES)
    angle = (turned * q % fine) * (2.0 * math.pi / fine)
    return np.concatenate([np.cos(angle), np.sin(angle)], axis=2).astype(np.float32)


def lane_matrix():
    fine = OUTER * LANES
    q = np.arange(LANES)
    angle = (q[:, None] * q[None, :] % LANES) * (2.0 * math.pi / LANES)
    cos, sin = np.cos(angle), np.sin(angle)
    return (np.block([[cos, -sin], [sin, cos]]) * fine**-0.5).astype(np.float32)


def add(x, y):
    return (x[0] + y[0], x[1] + y[1])


def sub(x, y):
    return (x[0] - y[0], x[1] - y[1])


def minus_i(x):
    return (x[1], -x[0])


def turn(x, step, count):
    step %= count
    if step == 0:
        return x
    if 4 * step == count:
        return minus_i(x)
    if 8 * step == count:
        half = math.sqrt(0.5)
        return ((x[0] + x[1]) * half, (x[1] - x[0]) * half)
    if 8 * step == 3 * count:
        half = math.sqrt(0.5)
        return ((x[1] - x[0]) * half, (x[0] + x[1]) * -half)
    cos, sin = math.cos(2 * math.pi * step / count), math.sin(2 * math.pi * step / count)
    return (x[0] * cos + x[1] * sin, x[1] * cos - x[0] * sin)


def four(x):
    even, odd = add(x[0], x[2]), sub(x[0], x[2])
    other, last = add(x[1], x[3]), minus_i(sub(x[1], x[3]))
    return [add(even, other), add(odd, last), sub(even, other), sub(odd, last)]


def eight(x):
    even, odd = four(x[0::2]), four(x[1::2])
    odd = [turn(value, k, 8) for k, value in enumerate(odd)]
    return [add(e, o) for e, o in zip(even, odd)] + [sub(e, o) for e, o in zip(even, odd)]


def bit_of(value, bit):
    return lax.rem(lax.div(value, 1 << bit), 2)


def top_bit(count):
    return count.bit_length() - 1


def hops(count):
    return [0] + sorted(range(2, count, 2), key=lambda hop: (-top_bit(hop), hop))


def frame_loads(frame_count):
    bounds = [0] + list(range(5, frame_count, 7)) + [frame_count]
    return list(zip(bounds[:-1], bounds[1:]))


def spectra_kernel(chan_count, spectra_count, volt_hbm, taps_hbm, table_hbm, *refs):
    outs, scratch = refs[:-10], refs[-10:]
    volt_ref, taps_ref, table_ref, matrix_ref = scratch[:4]
    filtered, first, last, pieces, volt_sems, table_sems = scratch[4:]
    tap_count, fine = taps_ref.shape
    frame_count = spectra_count + tap_count - 1
    loads = frame_loads(frame_count)
    volt_copies = []
    for at, (begin, end) in enumerate(loads):
        span = pl.ds(begin * fine, (end - begin) * fine)
        volt_copies.append(
            pltpu.make_async_copy(
                volt_hbm.at[:, :, span], volt_ref.at[:, :, span], volt_sems.at[at]
            )
        )
    table_copies = [
        pltpu.make_async_copy(source, target, table_sems.at[at])
        for at, (source, target) in enumerate(
            [(taps_hbm, taps_ref), (table_hbm, table_ref)]
        )
    ]
    volt_copies[0].start()
    table_copies[0].start()
    for copy in volt_copies[1:]:
        copy.start()
    table_copies[1].start()
    for at, (begin, end) in enumerate(loads):
        if at == 0:
            table_copies[0].wait()
        volt_copies[at].wait()

        def filter_column(p, carry, begin=begin, end=end):
            column = pl.multiple_of(p * LANES, LANES)
            taps = {}
            for t in range(max(0, begin - spectra_count + 1), min(tap_count, end)):
                taps[t] = taps_ref[pl.ds(t, 1), pl.ds(column, LANES)]
            for part in range(2):
                sums = {}
                for frame in range(begin, end):
                    lane = pl.multiple_of(frame * fine + column, LANES)
                    values = volt_ref[part, :, pl.ds(lane, LANES)].astype(jnp.float32)
                    for s in range(spectra_count):
                        if 0 <= frame - s < tap_count:
                            term = taps[frame - s] * values
                            if s not in sums and frame > s:
                                sums[s] = filtered[s, part, p]
                            sums[s] = sums[s] + term if s in sums else term
                for s, total in sums.items():
                    filtered[s, part, p] = total
            return carry

        lax.fori_loop(0, OUTER, filter_column, 0, unroll=8)
    table_copies[1].wait()
    table = table_ref[pl.ds(0, 2 * LANES), :]
    matrix_ref[0] = table.astype(jnp.bfloat16)
    matrix_ref[1] = (table - matrix_ref[0].astype(jnp.float32)).astype(jnp.bfloat16)

    def transform(s, carry):
        for a in range(8):
            values = four([(filtered[s, 0, a + 8 * b], filtered[s, 1, a + 8 * b]) for b in range(4)])
            for r in range(4):
                real, imag = turn(values[r], a * r, OUTER)
                first[0, r, a] = real
                first[1, r, a] = imag
        odd = s % 2
        for r in range(4):
            values = eight([(first[0, r, a], first[1, r, a]) for a in range(8)])
            highs, lows = [], []
            for t in range(8):
                k1 = r + 4 * t
                factors = table_ref[pl.ds(2 * LANES + odd * OUTER + k1, 1), :]
                cos, sin = factors[:, :LANES], factors[:, LANES:]
                real, imag = values[t]
                row = jnp.concatenate([real * cos + imag * sin, imag * cos - real * sin], axis=1)
                high = row.astype(jnp.bfloat16)
                highs.append(high)
                lows.append((row - high.astype(jnp.float32)).astype(jnp.bfloat16))
            high = jnp.concatenate(highs, axis=0)
            low = jnp.concatenate(lows, axis=0)
            dot = functools.partial(jnp.dot, preferred_element_type=jnp.float32)
            result = dot(high, matrix_ref[0]) + (dot(low, matrix_ref[0]) + dot(high, matrix_ref[1]))
            result = result.astype(jnp.bfloat16)
            for t in range(8):
                rows = result[t * ROWS : (t + 1) * ROWS]
                last[s, 0, r + 4 * t] = rows[:, :LANES]
                last[s, 1, r + 4 * t] = rows[:, LANES:]
        return carry


    lane = lax.broadcasted_iota(jnp.int32, (ROWS, LANES), 1)
    bits = [(lane >> bit) & 1 == 1 for bit in range(7)]
    group_count = pieces.shape[1]

    def regroup(part, pair):
        even = [last[2 * pair, part, k1] for k1 in range(OUTER)]
        odd = [last[2 * pair + 1, part, k1] for k1 in range(OUTER)]
        mixed = [
            [jnp.where(bits[1], odd[v], even[v]) for v in range(OUTER)],
            [jnp.where(bits[1], even[v], odd[v - 1]) for v in range(OUTER)],
        ]
        for which in range(2):
            tiles = [mixed[which][-v % OUTER] for v in range(OUTER)]
            for bit in range(5):
                tiles = [
                    jnp.where(bits[2 + bit], tiles[v - (1 << bit)], tiles[v])
                    for v in range(OUTER)
                ]
            for u in range(OUTER):
                chan, group = divmod(2 * u + which, group_count)
                pieces[chan, group, part * (spectra_count // 2) + pair] = tiles[u]

    for s in range(spectra_count):
        transform(s, 0)
        if s % 2:
            regroup(0, s // 2)
            regroup(1, s // 2)

    own = lax.axis_index("chan")
    top = bit_of(lax.axis_index("inp"), top_bit(lax.axis_size("inp")) - 1)
    half = group_count // 2
    moving, other = pl.ds((1 - top) * half, half), pl.ds(top * half, half)
    own_moving, own_other, *direct, held, relay_moving, relay_other = outs
    own_moving[...] = pieces[own, moving]
    own_other[...] = pieces[own, other]
    for index, hop in enumerate(hops(chan_count)):
        chan = jnp.bitwise_xor(own, hop)
        if index:
            direct[index - 1][...] = pieces[chan, moving]
            held[index - 1] = pieces[chan, other]
        relay_moving[index] = pieces[jnp.bitwise_xor(chan, 1), moving]
        relay_other[index] = pieces[jnp.bitwise_xor(chan, 1), other]


def spectra_pieces(voltages, filter_taps, chan_count):
    tap_count, fine = filter_taps.shape
    signals = voltages.shape[1]
    spectra_count = voltages.shape[2] // fine - tap_count + 1
    padded = -signals % ROWS
    if padded:
        voltages = jnp.pad(voltages, ((0, 0), (0, padded), (0, 0)))
    group_count = fine // AVG // chan_count
    slices = spectra_count
    piece = (group_count, slices, ROWS, LANES)
    part = (group_count // 2, slices, ROWS, LANES)
    half_count = chan_count // 2
    shapes = [part] * (half_count + 1) + [(half_count - 1,) + part] + [(half_count,) + part] * 2
    table = np.concatenate([lane_matrix(), twiddle_table().reshape(-1, 2 * LANES)])
    outs = pl.pallas_call(
        functools.partial(spectra_kernel, chan_count, spectra_count),
        out_shape=[jax.ShapeDtypeStruct(shape, jnp.bfloat16) for shape in shapes],
        in_specs=[pl.BlockSpec(memory_space=pltpu.HBM)] * 3,
        out_specs=[pl.BlockSpec(memory_space=pltpu.VMEM)] * len(shapes),
        scratch_shapes=[
            pltpu.VMEM(voltages.shape, jnp.bfloat16),
            pltpu.VMEM(filter_taps.shape, jnp.float32),
            pltpu.VMEM(table.shape, jnp.float32),
            pltpu.VMEM((2, 2 * LANES, 2 * LANES), jnp.bfloat16),
            pltpu.VMEM((spectra_count, 2, OUTER, ROWS, LANES), jnp.float32),
            pltpu.VMEM((2, 4, 8, ROWS, LANES), jnp.float32),
            pltpu.VMEM((spectra_count, 2, OUTER, ROWS, LANES), jnp.bfloat16),
            pltpu.VMEM((chan_count,) + piece, jnp.bfloat16),
            pltpu.SemaphoreType.DMA((len(frame_loads(spectra_count + tap_count - 1)),)),
            pltpu.SemaphoreType.DMA((2,)),
        ],
        compiler_params=pltpu.CompilerParams(vmem_limit_bytes=53 * MIB),
        name="spectra",
    )(voltages, filter_taps, jnp.asarray(table))
    outs = [out[..., :signals, :] for out in outs]
    return outs[:2] + [outs[2:-3]] + outs[-3:]


def vmem_call(name, kernel, out_shapes, operands, after=(), cost=None, aliases=None):
    count = len(operands)
    operands = list(operands) + list(after)

    def body(*refs):
        kernel(*refs[:count], *refs[len(operands) :])

    return pl.pallas_call(
        body,
        out_shape=[jax.ShapeDtypeStruct(shape, jnp.bfloat16) for shape in out_shapes],
        in_specs=[pl.BlockSpec(memory_space=pltpu.VMEM)] * count
        + [pl.BlockSpec(memory_space=pl.ANY)] * len(after),
        out_specs=[pl.BlockSpec(memory_space=pltpu.VMEM)] * len(out_shapes),
        compiler_params=pltpu.CompilerParams(vmem_limit_bytes=8 * MIB),
        cost_estimate=cost,
        input_output_aliases=aliases or {},
        name=name,
    )(*operands)


def split_kernel(relayed, *outs):
    for index, out in enumerate(outs):
        out[...] = relayed[index]


def hand_on_kernel(held, relayed, *outs):
    for index, out in enumerate(outs):
        out[0] = held[index]
        out[1] = relayed[index + 1]


def lay(out, pieces):
    count = len(pieces)
    if count == 1:
        out[...] = pieces[0][...]
        return
    own = lax.axis_index("chan")
    rows = out.shape[2] // count
    for hop, piece in zip(hops(2 * count), pieces):
        source = lax.div(jnp.bitwise_xor(own, hop), 2)
        span = pl.ds(pl.multiple_of(source * rows, rows), rows)
        out[:, :, span, :] = piece[...]


def lay_kernel(*refs):
    lay(refs[-1], refs[:-1])


def lay_rest_kernel(rest_count, near_moving, far_moving, own_other, relayed, *refs):
    rest, outs = refs[:rest_count], refs[rest_count:]
    near = [own_other] + [value.at[0] for value in rest]
    far = [relayed.at[0]] + [value.at[1] for value in rest]
    lay_other_kernel(len(near), near_moving, far_moving, *near, *far, *outs)


def lay_other_kernel(piece_count, near_moving, far_moving, *refs):
    near, far = refs[:piece_count], refs[piece_count : 2 * piece_count]
    near_other, far_other, *sends = refs[2 * piece_count :]
    lay(near_other, near)
    lay(far_other, far)
    block = lax.axis_index("inp")
    top = bit_of(block, len(sends))
    for bit, out in enumerate(sends):
        same = bit_of(block, bit) == top

        @pl.when(same)
        def _(out=out):
            out[0] = near_moving[...]
            out[1] = far_moving[...]

        @pl.when(jnp.logical_not(same))
        def _(out=out):
            out[0] = near_other[...]
            out[1] = far_other[...]


def products(left, right):
    slices, rows, _ = left.shape

    def operand(values):
        part = slices // 2
        real = jnp.concatenate([values[i] for i in range(part)], axis=1)
        imag = jnp.concatenate([values[i] for i in range(part, slices)], axis=1)
        return jnp.concatenate([real, imag], axis=0)

    contract = (((1,), (1,)), ((), ()))
    all_parts = lax.dot_general(
        operand(left), operand(right), contract, preferred_element_type=jnp.float32
    )
    scale = 2.0 / (slices * LANES)
    real = all_parts[:rows, :rows] + all_parts[rows:, rows:]
    imag = all_parts[rows:, :rows] - all_parts[:rows, rows:]
    return real * scale, imag * scale


def fill(target, parts, chan_count):
    if len(parts) == 1:
        target[...] = parts[0][...]
        return
    for parity, part in enumerate(parts):
        fill_parity(target, part, chan_count, parity)


def fill_parity(target, part, chan_count, parity):
    own = lax.rem(lax.axis_index("chan"), 2)
    first = own if parity == 0 else 1 - own
    rows = target.shape[2] // chan_count
    for source in range(chan_count // 2):
        span = pl.ds(pl.multiple_of((2 * source + first) * rows, rows), rows)
        target[:, :, span, :] = part[:, :, pl.ds(source * rows, rows), :]


def round_of(pairing_ref, mask):
    rounds = lax.broadcasted_iota(jnp.int32, pairing_ref.shape, 1)
    return jnp.max(jnp.where(pairing_ref[...] == mask, rounds, 0))


def first_kernel(chan_count, block_bits, count, mask, pairing_ref, *refs):
    inputs = [refs[at * count : (at + 1) * count] for at in range(3)]
    block, autos_hbm, vis_hbm, partner, autos, vis, sems, vis_sems = refs[3 * count :]
    half = block.shape[1]
    top = bit_of(lax.axis_index("inp"), block_bits - 1)
    copies = []

    def store(source, target, sem):
        copy = pltpu.make_async_copy(source, target, sem)
        copy.start()
        copies.append(copy)

    for slot in range(2):
        fill(block.at[slot], inputs[slot], chan_count)
        for group in range(half):
            rows = block[slot, group]
            autos[0, slot, group], autos[1, slot, group] = products(rows, rows)
        place = pl.ds(half * (slot * top + (1 - slot) * (1 - top)), half)
        for part in range(2):
            store(autos.at[part, slot], autos_hbm.at[part, place], sems.at[part, slot])
    fill(partner, inputs[2], chan_count)
    place = round_of(pairing_ref, mask)
    for group in range(half):
        vis[0, group], vis[1, group] = products(block[1, group], partner[group])
        store(vis.at[:, group], vis_hbm.at[:, place, group], vis_sems.at[group])
    for copy in copies:
        copy.wait()


def first_call(pairing, operands, mask, chan_count, block_bits):
    half, slices, rows = operands[0].shape[:3]
    count = len(operands) // 3
    rows *= count
    auto_shape = (2, 2, half, rows, rows)
    block_shape = (2, half, slices, rows, LANES)
    return pl.pallas_call(
        functools.partial(first_kernel, chan_count, block_bits, count, mask),
        out_shape=[
            jax.ShapeDtypeStruct(block_shape, jnp.bfloat16),
            jax.ShapeDtypeStruct((2, 2 * half, rows, rows), jnp.float32),
            jax.ShapeDtypeStruct((2, pairing.shape[1], half, rows, rows), jnp.float32),
        ],
        in_specs=[pl.BlockSpec(memory_space=pltpu.VMEM)] * (1 + len(operands)),
        out_specs=[pl.BlockSpec(memory_space=pltpu.VMEM)]
        + [pl.BlockSpec(memory_space=pltpu.HBM)] * 2,
        scratch_shapes=[
            pltpu.VMEM(block_shape[1:], jnp.bfloat16),
            pltpu.VMEM(auto_shape, jnp.float32),
            pltpu.VMEM((2, half, rows, rows), jnp.float32),
            pltpu.SemaphoreType.DMA((2, 2)),
            pltpu.SemaphoreType.DMA((half,)),
        ],
        compiler_params=pltpu.CompilerParams(vmem_limit_bytes=12 * MIB),
        cost_estimate=pl.CostEstimate(flops=1 << 20, bytes_accessed=4 << 20, transcendentals=0),
        name="correlate_first",
    )(pairing, *operands)


def parts_of(layout, refs):
    found, at = [], 0
    for kind in layout:
        if kind == "stack":
            found.append([refs[at].at[0], refs[at].at[1]])
            at += 1
        else:
            count = 2 if kind == "pair" else 1
            found.append(list(refs[at : at + count]))
            at += count
    return found


def fill_parity_kernel(chan_count, parity, *refs):
    for index, part in enumerate(refs[: -1 - parity]):
        fill_parity(refs[-1].at[index], part, chan_count, parity)


def fill_kernel(*refs):
    for index, part in enumerate(refs[:-1]):
        refs[-1][index] = part[...]


def cross_kernel(chan_count, block_bits, early, late, layout, pairing_ref, block, filled, *refs):
    inputs, refs = refs[: -len(SCRATCH) - 1], refs[-len(SCRATCH) :]
    vis_hbm, others, vis, vis_sems = refs
    own = lax.axis_index("inp")
    top = bit_of(own, block_bits - 1)
    half = block.shape[1]
    for index, parts in enumerate(parts_of(layout, inputs)):
        fill(others.at[index], parts, chan_count)
    partners = [(mask, filled.at[at]) for at, mask in enumerate(early)]
    partners += [(mask, others.at[at]) for at, mask in enumerate(late)]
    copies = []
    for index, (mask, other) in enumerate(partners):
        bit = top_bit(mask)
        slot = 1
        if bit != block_bits - 1:
            slot = (bit_of(own, bit) == top).astype(jnp.int32)
        place = round_of(pairing_ref, mask)
        for group in range(half):
            vis[0, index, group], vis[1, index, group] = products(block[slot, group], other[group])
            copy = pltpu.make_async_copy(
                vis.at[:, index, group], vis_hbm.at[:, place, group], vis_sems.at[index, group]
            )
            copy.start()
            copies.append(copy)
    for copy in copies:
        copy.wait()


SCRATCH = ("vis_hbm", "others", "vis", "vis_sems")


def cross_call(pairing, block, visibilities, received, early, late, chan_count, block_bits):
    _, half, slices, rows, _ = block.shape
    filled_shape = (len(early),) + block.shape[1:]
    cost = functools.partial(pl.CostEstimate, transcendentals=0)
    if received[early[0]][0] == "pair":
        filled = []
        for parity in range(2):
            filled = vmem_call(
                "fill_far" if parity else "fill_near",
                functools.partial(fill_parity_kernel, chan_count, parity),
                [filled_shape],
                [received[mask][1][parity] for mask in early] + list(filled),
                cost=cost(flops=FILL_FLOPS[parity], bytes_accessed=1 << 20),
                aliases={len(early): 0} if parity else None,
            )
    else:
        filled = vmem_call(
            "fill", fill_kernel, [filled_shape], [received[mask][1][0] for mask in early]
        )
    (filled,) = filled
    layout = tuple(received[mask][0] for mask in late)
    operands = [value for mask in late for value in received[mask][1]]
    count = len(early) + len(late)
    vis_shape = (2, count, half, rows, rows)
    return pl.pallas_call(
        functools.partial(cross_kernel, chan_count, block_bits, early, late, layout),
        out_shape=jax.ShapeDtypeStruct(visibilities.shape, jnp.float32),
        in_specs=[pl.BlockSpec(memory_space=pltpu.VMEM)] * (3 + len(operands))
        + [pl.BlockSpec(memory_space=pltpu.HBM)],
        out_specs=pl.BlockSpec(memory_space=pltpu.HBM),
        input_output_aliases={3 + len(operands): 0},
        scratch_shapes=[
            pltpu.VMEM((len(late), half, slices, rows, LANES), jnp.bfloat16),
            pltpu.VMEM(vis_shape, jnp.float32),
            pltpu.SemaphoreType.DMA(vis_shape[1:3]),
        ],
        compiler_params=pltpu.CompilerParams(vmem_limit_bytes=16 * MIB),
        cost_estimate=pl.CostEstimate(
            flops=16 * count * half * rows * rows * slices * LANES,
            bytes_accessed=4 << 20,
            transcendentals=0,
        ),
        name="cross",
    )(pairing, block, filled, *operands, visibilities)


def on_device(voltages, filter_taps, pairing):
    pairing = pairing[None, :]
    chan_count = lax.axis_size("chan")
    inp_count = lax.axis_size("inp")
    block_bits = top_bit(inp_count)
    own_chan = lax.axis_index("chan")
    signals = voltages.shape[1]

    def exchange(value, axis, mask):
        count = lax.axis_size(axis)
        return lax.ppermute(value, axis, [(i, i ^ mask) for i in range(count)])

    evens = hops(chan_count)[1:]

    def along(values):
        return [exchange(value, "chan", k) for value, k in zip(values, evens)]

    own_moving, own_other, direct, held, relay_moving, relay_other = spectra_pieces(
        voltages, filter_taps, chan_count
    )
    part = own_moving.shape
    half = part[0]
    relay_moving = exchange(relay_moving, "chan", 1)
    direct = along(direct)
    relay_other = exchange(relay_other, "chan", 1)
    far_own, *onward = vmem_call(
        "split", split_kernel, [part] * (chan_count // 2), [relay_moving]
    )
    onward = along(onward)
    near, far = [own_moving] + direct, [far_own] + onward
    laid = part[:2] + (chan_count // 2 * signals, LANES)
    whole_tiles = signals % ROWS == 0
    top_mask = inp_count // 2
    if not whole_tiles:
        ordered = np.argsort(hops(chan_count))
        sources = jnp.bitwise_xor(own_chan // 2, jnp.arange(chan_count // 2))

        def merge(parts):
            parts = [parts[at] for at in ordered]
            return jnp.take(jnp.stack(parts, axis=2), sources, axis=2).reshape(laid)

        near, far = [merge(near)], [merge(far)]
    (near,) = vmem_call("near", lay_kernel, [laid], near)
    crossed = [exchange(near, "inp", top_mask)]
    (far,) = vmem_call("far", lay_kernel, [laid], far)
    crossed.append(exchange(far, "inp", top_mask))
    rest = vmem_call(
        "hand_on",
        hand_on_kernel,
        [(2,) + part] * len(evens),
        [held, relay_other],
        [direct[0]],
    )
    rest = along(rest)
    if whole_tiles:
        other_kernel = functools.partial(lay_rest_kernel, len(evens))
        others = [own_other, relay_other] + rest
    else:
        other_kernel = functools.partial(lay_other_kernel, 1)
        others = [
            merge([own_other] + [value[0] for value in rest]),
            merge([relay_other[0]] + [value[1] for value in rest]),
        ]
    near_other, far_other, *sends = vmem_call(
        "other",
        other_kernel,
        [laid] * 2 + [(2,) + laid] * (block_bits - 1),
        [near, far] + others,
    )
    masks = list(range(1, inp_count))
    received = {top_mask: ("pair", crossed)}
    for mask in masks:
        bit = top_bit(mask)
        if mask == top_mask:
            continue
        if mask > 1 and mask % 2:
            kind, values = received[mask - 1]
            received[mask] = (kind, [exchange(value, "inp", 1) for value in values])
        else:
            kind, values = "pair", [near, far]
            if bit != block_bits - 1:
                kind, values = "stack", [sends[bit]]
            received[mask] = (kind, [exchange(value, "inp", mask) for value in values])
    block = [("pair", [near, far]), ("pair", [near_other, far_other])]
    if not whole_tiles:
        parities = jnp.bitwise_xor(own_chan % 2, jnp.arange(2))

        def interleave(entry):
            kind, values = entry
            if kind == "stack":
                values = [values[0][0], values[0][1]]
            shaped = [value.reshape(half, -1, chan_count // 2, signals, LANES) for value in values]
            ordered = jnp.take(jnp.stack(shaped, axis=3), parities, axis=3)
            return ("whole", [ordered.reshape(half, -1, chan_count * signals, LANES)])

        block = [interleave(entry) for entry in block]
        received = {mask: interleave(entry) for mask, entry in received.items()}
    early = [mask for mask in masks if mask > top_mask]
    late = [mask for mask in masks if mask < top_mask]
    rows, autos, visibilities = first_call(
        pairing,
        [value for _, values in block + [received[top_mask]] for value in values],
        top_mask,
        chan_count,
        block_bits,
    )
    visibilities = cross_call(
        pairing, rows, visibilities, received, early, late, chan_count, block_bits
    )
    return (visibilities, autos)


def solution(mesh):
    in_specs = (P(None, ("inp", "chan"), None), P(), P())
    out_specs = (P(None, None, "chan", "inp", None), P(None, "chan", "inp", None))
    return jax.shard_map(
        on_device, mesh=mesh, in_specs=in_specs, out_specs=out_specs, check_vma=False
    )
```
